512 devices in a mesh: normal: 16 (over z), span: 8 (over x, core), stream: 4 (over y).
Axes of the slice: x: 4, y: 4, z: 16, core: 2. Of those that a mesh axis runs over, the one named last changes fastest.
Arguments:
- iterate: float32 [768, 5, 8, 512], P('normal', None, 'span', 'stream'), may hold values from -6 to 6
- source: float32 [768, 5, 8, 512], P('normal', None, 'span', 'stream'), may hold values from -6 to 6
- pivot: float32 [768, 5, 5, 8, 512], P('normal', None, None, 'span', 'stream'), as said below
- lower: float32 [768, 5, 5, 8, 512], P('normal', None, None, 'span', 'stream'), as said below
- upper: float32 [768, 5, 5, 8, 512], P('normal', None, None, 'span', 'stream'), as said below
- coupling: float32 [4, 768, 5, 5, 8, 512], P(None, 'normal', None, None, 'span', 'stream'), may hold values from -0.6 to 0.6
- iblank: int32 [768, 8, 512], P('normal', 'span', 'stream'), may hold values from 0 to 2
- donor: int32 [768, 8, 512], P('normal', 'span', 'stream'), may hold values from 0 to 6143
Outputs:
- smoothed: float32 [768, 5, 8, 512], P('normal', None, 'span', 'stream')
The draws below stay inside these ranges and needn't reach their ends.
Inputs may be any that keep to these rules, and one draw needn't show every extreme that they name: `donor`: an offset within a tile of 48 x 1 x 128 points. pivot blocks are full 5x5 blocks. lower and upper factor blocks are full 5x5 blocks; the recurrences stay bounded. upper factor blocks are full 5x5 blocks.
All inputs are finite; a program needn't handle non-finite values.
Results may differ from the reference program's by a relative error of at most 0.00018.
Values sent between devices are 32-bit elements; how exact they have to be, the bound alone decides.
No kernel may reach another device: no remote copies, remote signals or barrier semaphores. Data moves between devices by JAX's collectives and lax.ppermute only.
A program may use at most 64 MiB of HBM per device.

```python
import math
import jax
import jax.numpy as jnp
from jax import lax

CN = 48
SP = 1
ST = 128
COMP = 5
SWEEPS = 2
LINE_POINTS = 768
SPAN = 8
STREAM = 512


def factored_block_list(key, lower_rate, higher_rate, include_spike_events, diagonal_polarity):
    rate_draw_key, perturbation_key, spike_event_key, displacement_key = jax.random.split(key, 4)
    eye = jnp.eye(5, dtype=jnp.float32)[None, :, :, None, None]
    rate = jnp.exp(jax.random.uniform(rate_draw_key, (1, 5, 1, SPAN, STREAM), jnp.float32, math.log(lower_rate), math.log(higher_rate)))
    jitter = jax.random.uniform(perturbation_key, (LINE_POINTS, 5, 1, SPAN, STREAM), jnp.float32, 0.7, 1.4)
    retain_flags = jnp.exp(-rate * jitter)
    if include_spike_events:
        spike_event = jax.random.uniform(spike_event_key, (LINE_POINTS, 1, 1, 1, 1), jnp.float32) < 4.0 / LINE_POINTS
        retain_flags = jnp.where(spike_event, retain_flags * 0.6, retain_flags)
    off = 0.01 * jax.random.normal(displacement_key, (LINE_POINTS, 5, 5, SPAN, STREAM), jnp.float32)
    return diagonal_polarity * retain_flags * eye + off * (1.0 - eye)


def draw_pivot(key, part):
    key_diag, displacement_key = jax.random.split(jax.random.fold_in(key, 11))
    eye = jnp.eye(5, dtype=jnp.float32)[None, :, :, None, None]
    diag = jnp.exp(jax.random.uniform(key_diag, (LINE_POINTS, 5, 1, SPAN, STREAM), jnp.float32, math.log(0.004), math.log(0.02)))
    off = 0.002 * jax.random.normal(displacement_key, (LINE_POINTS, 5, 5, SPAN, STREAM), jnp.float32)
    return diag * eye + off * (1.0 - eye)


def draw_lower(key, part):
    return factored_block_list(jax.random.fold_in(key, 23), 0.3 / LINE_POINTS, 1.0 / 30.0, True, -1.0)


def draw_upper(key, part):
    return factored_block_list(jax.random.fold_in(key, 37), 0.3 / LINE_POINTS, 1.0 / 30.0, True, 1.0)


def touch_ends(array, own_key, low, largest):
    longest = array.shape.index(max(array.shape))
    spots = []
    for shift in (0, 1):
        where = [jax.random.randint(jax.random.fold_in(own_key, axis), (), 0, length) for axis, length in enumerate(array.shape)]
        where[longest] = (where[longest] + shift) % array.shape[longest]
        spots.append(tuple(where))
    return array.at[spots[0]].set(low).at[spots[1]].set(largest)


def block_scale(own_key, extent, shards, smallest, top_value):
    gain = 1.0
    for axis_at, shards_of in shards:
        heights = jax.random.uniform(jax.random.fold_in(jax.random.fold_in(own_key, 6), axis_at), (shards_of,), jnp.float32, smallest / len(shards), top_value / len(shards))
        gain = gain * jnp.repeat(jnp.exp(heights), extent[axis_at] // shards_of).reshape((-1,) + (1,) * (len(extent) - 1 - axis_at))
    return gain


def centred(own_key, extent, deviation, most, pieces=(), held_as=jnp.bfloat16):
    values = jax.random.normal(own_key, extent, jnp.float32) * deviation
    if len(pieces) > 0:
        values = block_scale(own_key, extent, pieces, -0.22, 0.18) * values
    return jnp.clip(values, min=-most, max=most).astype(held_as)


def setup_inputs(seed: int = 0) -> dict:
    keys = jax.random.split(jax.random.key(seed), 9)
    return {
        "iterate": centred(keys[0], (LINE_POINTS, COMP, SPAN, STREAM), 1.0, 6.0, ((0, 16), (2, 8), (3, 4)), jnp.float32),
        "source": centred(keys[1], (LINE_POINTS, COMP, SPAN, STREAM), 1.0, 6.0, ((0, 16), (2, 8), (3, 4)), jnp.float32),
        "pivot": draw_pivot(jax.random.fold_in(keys[8], 71), 0),
        "lower": draw_lower(jax.random.fold_in(keys[8], 71), 0),
        "upper": draw_upper(jax.random.fold_in(keys[8], 71), 0),
        "coupling": centred(keys[5], (4, LINE_POINTS, COMP, COMP, SPAN, STREAM), 0.1, 0.6, ((1, 16), (4, 8), (5, 4)), jnp.float32),
        "iblank": touch_ends(jax.random.randint(keys[6], (LINE_POINTS, SPAN, STREAM), 0, 3), jax.random.fold_in(keys[6], 1), 0, 2).astype(jnp.int32),
        "donor": touch_ends(jax.random.randint(keys[7], (LINE_POINTS, SPAN, STREAM), 0, CN * SP * ST), jax.random.fold_in(keys[7], 1), 0, (CN * SP * ST) - 1).astype(jnp.int32),
    }


def one_sweep(x, source, pivot, lower, upper, coupling, iblank, donor):
    near = [jnp.roll(x, 1, axis=2), jnp.roll(x, -1, axis=2), jnp.roll(x, 1, axis=3), jnp.roll(x, -1, axis=3)]
    couple = jnp.zeros_like(x)
    for direc in range(4):
        couple = couple + jnp.sum(coupling[direc] * near[direc][:, :, None], axis=1)
    line_pos = jnp.arange(LINE_POINTS, dtype=jnp.int32)[:, None, None]
    span_pos = jnp.arange(SPAN, dtype=jnp.int32)[None, :, None]
    strm_pos = jnp.arange(STREAM, dtype=jnp.int32)[None, None, :]
    line_idx = (line_pos // CN) * CN + donor // (SP * ST)
    span_idx = (span_pos // SP) * SP + (donor // ST) % SP
    strm_idx = (strm_pos // ST) * ST + donor % ST
    donated = jnp.transpose(x, (0, 2, 3, 1))[line_idx, span_idx, strm_idx]
    donated = jnp.transpose(donated, (0, 3, 1, 2))
    flag = iblank[:, None]
    rhs = jnp.where(flag == 0, 0.0, source - couple + jnp.where(flag == 2, donated, 0.0))
    scaled = jnp.sum(pivot * rhs[:, None], axis=2)

    def forward(state, inputs):
        term, block = inputs
        state = term - jnp.sum(block * state[None], axis=1)
        return state, state

    start = jnp.zeros((COMP, SPAN, STREAM), jnp.float32)
    _, ys = lax.scan(forward, start, (scaled, lower))

    def backward(state, inputs):
        term, block = inputs
        state = term - jnp.sum(block * state[None], axis=1)
        return state, state

    _, xs = lax.scan(backward, start, (ys, upper), reverse=True)
    return xs


def reference(iterate, source, pivot, lower, upper, coupling, iblank, donor):
    x = iterate
    for sweep in range(SWEEPS):
        x = one_sweep(x, source, pivot, lower, upper, coupling, iblank, donor)
    return x
```

```python
import functools

import jax
import jax.numpy as jnp
from jax import lax
from jax.experimental import pallas as pl
from jax.experimental.pallas import tpu as pltpu
from jax.sharding import PartitionSpec as P

COMP = 5
BLOCK = COMP * COMP
PIECES = 8
LANES = 128
STEPS = 6
POINTS = PIECES * STEPS
SIZES = range(COMP)
FWD0, FWD1, FWD2, BWD0, BWD1, BWD2, FOLD, HEAD, FROM_Y, FROM_X = range(10)
MAPS = 10
ROWS = 3 * BLOCK
VALUES = 2 * COMP
PADDED = 88
VMEM = pl.BlockSpec(memory_space=pltpu.VMEM)


def vector_at(ref, step):
    return [ref[pl.ds(step * COMP + c, PIECES, stride=STEPS * COMP), :] for c in SIZES]


def block_at(ref, step, base=0):
    start = base + step * BLOCK
    return [
        [ref[pl.ds(start + c * COMP + e, PIECES, stride=STEPS * BLOCK), :] for e in SIZES]
        for c in SIZES
    ]


def packed_at(ref, step):
    return [ref[pl.ds((step * COMP + c) * PIECES, PIECES), :] for c in SIZES]


def put_packed(ref, step, value):
    for c in SIZES:
        ref[pl.ds((step * COMP + c) * PIECES, PIECES), :] = value[c]


def map_at(ref, which):
    return [
        [ref[pl.ds(((which * COMP + c) * COMP + e) * PIECES, PIECES), :] for e in SIZES]
        for c in SIZES
    ]


def put_map(ref, which, value):
    for c in SIZES:
        for e in SIZES:
            ref[pl.ds(((which * COMP + c) * COMP + e) * PIECES, PIECES), :] = value[c][e]


def total(terms):
    while len(terms) > 1:
        terms = [sum(terms[k : k + 2][1:], terms[k]) for k in range(0, len(terms), 2)]
    return terms[0]


def times(block, vector):
    return [total([block[c][e] * vector[e] for e in SIZES]) for c in SIZES]


def product(left, right):
    return [
        [total([left[c][k] * right[k][e] for k in SIZES]) for e in SIZES] for c in SIZES
    ]


def each(function, *maps):
    return [[function(*(m[c][e] for m in maps)) for e in SIZES] for c in SIZES]


def add(left, right):
    return [a + b for a, b in zip(left, right)]


def less(left, right):
    return [a - b for a, b in zip(left, right)]


def moved(value, steps):
    return pltpu.roll(value, steps % PIECES, 0)


def donate(x_ref, donor_ref, donated_ref):
    lanes, rows = [], []
    for step in range(STEPS):
        place = donor_ref[pl.ds(step, PIECES, stride=STEPS), :]
        lanes.append(place & (LANES - 1))
        rows.append(place >> 7)

    def body(row, found):
        found = list(found)
        values = [
            jnp.broadcast_to(x_ref[pl.ds(row * COMP + c, 1), :], (PIECES, LANES)) for c in SIZES
        ]
        for step in range(STEPS):
            here = rows[step] == row
            for c in SIZES:
                picked = jnp.take_along_axis(
                    values[c], lanes[step], axis=1, mode="promise_in_bounds"
                )
                at = step * COMP + c
                found[at] = jnp.where(here, picked, found[at])
        return tuple(found)

    zero = jnp.zeros((PIECES, LANES), jnp.float32)
    found = lax.fori_loop(0, POINTS, body, (zero,) * (STEPS * COMP))
    for at in range(STEPS * COMP):
        donated_ref[pl.ds(at * PIECES, PIECES), :] = found[at]


def donate_kernel(x_ref, donor_ref, donated_ref):
    donate(x_ref, donor_ref, donated_ref)


def maps_kernel(lower_ref, upper_ref, maps_ref, whole_ref, local_ref):
    piece = lax.broadcasted_iota(jnp.int32, (PIECES, LANES), 0)
    one = jnp.ones((PIECES, LANES), jnp.float32)
    zero = jnp.zeros((PIECES, LANES), jnp.float32)
    eye = [[one if c == e else zero for e in SIZES] for c in SIZES]

    def pack(value):
        return tuple(value[c][e] for c in SIZES for e in SIZES)

    def unpack(flat):
        return [list(flat[c * COMP : (c + 1) * COMP]) for c in SIZES]

    first = each(lambda a: -a, block_at(lower_ref, 0))
    put_map(local_ref, 0, first)

    def forward(step, state):
        block = block_at(lower_ref, step)
        state = each(lambda a: -a, product(block, unpack(state)))
        put_map(local_ref, step, state)
        return pack(state)

    ahead = unpack(lax.fori_loop(1, STEPS, forward, pack(first)))

    def backward(count, carry):
        behind, fold = unpack(carry[:BLOCK]), unpack(carry[BLOCK:])
        step = STEPS - 1 - count
        block = block_at(upper_ref, step)
        behind = each(lambda a: -a, product(block, behind))
        fold = each(lambda a, b: a - b, map_at(local_ref, step), product(block, fold))
        return pack(behind) + pack(fold)

    last = block_at(upper_ref, STEPS - 1)
    start = pack(each(lambda a: -a, last)) + pack(map_at(local_ref, STEPS - 1))
    carry = lax.fori_loop(1, STEPS, backward, start)
    behind, fold = unpack(carry[:BLOCK]), unpack(carry[BLOCK:])
    put_map(maps_ref, FOLD, fold)

    window = ahead
    for level, shift in enumerate((1, 2, 4)):
        inside = piece >= shift
        put_map(maps_ref, FWD0 + level, each(lambda a: jnp.where(inside, a, 0.0), window))
        longer = product(window, each(lambda a: moved(a, shift), window))
        window = each(lambda a, b: jnp.where(inside, a, b), longer, window)
    head = each(lambda a, b: jnp.where(piece == 0, b, moved(a, 1)), window, eye)
    put_map(maps_ref, HEAD, head)
    for c in SIZES:
        for e in SIZES:
            whole_ref[pl.ds(c * COMP + e, 1), :] = window[c][e][PIECES - 1 :, :]

    window = behind
    response = product(fold, head)
    for level, shift in enumerate((1, 2, 4)):
        inside = piece < PIECES - shift
        masked = each(lambda a: jnp.where(inside, a, 0.0), window)
        put_map(maps_ref, BWD0 + level, masked)
        response = each(
            lambda a, b: a + b,
            response,
            product(masked, each(lambda a: moved(a, -shift), response)),
        )
        longer = product(window, each(lambda a: moved(a, -shift), window))
        window = each(lambda a, b: jnp.where(inside, a, b), longer, window)
    final = piece == PIECES - 1
    put_map(maps_ref, FROM_Y, each(lambda a: jnp.where(final, 0.0, moved(a, -1)), response))
    put_map(maps_ref, FROM_X, each(lambda a, b: jnp.where(final, b, moved(a, -1)), window, eye))
    for c in SIZES:
        for e in SIZES:
            at = c * COMP + e
            whole_ref[pl.ds(BLOCK + at, 1), :] = response[c][e][:1, :]
            whole_ref[pl.ds(2 * BLOCK + at, 1), :] = window[c][e][:1, :]


def solve_kernel(
    copies,
    x_ref,
    below_ref,
    above_ref,
    left_ref,
    right_ref,
    source_ref,
    pivot_ref,
    lower_ref,
    upper_ref,
    coupling_ref,
    iblank_ref,
    donated_ref,
    maps_ref,
    whole_ref,
    sent_ref,
    scaled_ref,
    starts_ref,
    states_ref,
):
    lane = lax.broadcasted_iota(jnp.int32, (PIECES, LANES), 1)
    piece = lax.broadcasted_iota(jnp.int32, (PIECES, LANES), 0)
    zero = jnp.zeros((PIECES, LANES), jnp.float32)

    def forward(step, state):
        x = vector_at(x_ref, step)
        before = [
            pltpu.roll(jnp.where(lane == LANES - 1, a, b), 1, 1)
            for a, b in zip(vector_at(left_ref, step), x)
        ]
        after = [
            pltpu.roll(jnp.where(lane == 0, a, b), LANES - 1, 1)
            for a, b in zip(vector_at(right_ref, step), x)
        ]
        near = [vector_at(below_ref, step), vector_at(above_ref, step), before, after]
        rhs = vector_at(source_ref, step)
        for direc in range(4):
            block = block_at(coupling_ref, step, direc * POINTS * BLOCK)
            for c in SIZES:
                rhs[c] = rhs[c] - total([block[e][c] * near[direc][e] for e in SIZES])
        flag = iblank_ref[pl.ds(step, PIECES, stride=STEPS), :]
        donated = packed_at(donated_ref, step)
        rhs = [
            jnp.where(flag == 0, 0.0, a + jnp.where(flag == 2, b, 0.0))
            for a, b in zip(rhs, donated)
        ]
        scaled = times(block_at(pivot_ref, step), rhs)
        put_packed(scaled_ref, step, scaled)
        state = less(scaled, times(block_at(lower_ref, step), state))
        put_packed(states_ref, step, state)
        return tuple(state)

    ahead = list(lax.fori_loop(0, STEPS, forward, (zero,) * COMP))

    def backward(count, state):
        step = STEPS - 1 - count
        y = packed_at(states_ref, step)
        return tuple(less(y, times(block_at(upper_ref, step), state)))

    behind = list(lax.fori_loop(0, STEPS, backward, (zero,) * COMP))

    for level, shift in enumerate((1, 2, 4)):
        ahead = add(ahead, times(map_at(maps_ref, FWD0 + level), [moved(a, shift) for a in ahead]))
    entry = [jnp.where(piece == 0, 0.0, moved(a, 1)) for a in ahead]
    behind = add(behind, times(map_at(maps_ref, FOLD), entry))
    for level, shift in enumerate((1, 2, 4)):
        behind = add(
            behind, times(map_at(maps_ref, BWD0 + level), [moved(a, -shift) for a in behind])
        )
    put_packed(starts_ref, 0, entry)
    put_packed(
        starts_ref, 1, [jnp.where(piece == PIECES - 1, 0.0, moved(a, -1)) for a in behind]
    )
    if whole_ref is not None:
        sent_ref[pl.ds(0, ROWS), :] = whole_ref[...]
        base = ROWS
        sent_ref[pl.ds(ROWS + VALUES, PADDED - ROWS - VALUES), :] = jnp.zeros(
            (PADDED - ROWS - VALUES, LANES), jnp.float32
        )
    else:
        base = 0
    for copy in range(copies):
        for c in SIZES:
            at = base + copy * VALUES + c
            sent_ref[pl.ds(at, 1), :] = ahead[c][PIECES - 1 :, :]
            sent_ref[pl.ds(at + COMP, 1), :] = behind[c][:1, :]


def solve_without(copies, *refs):
    solve_kernel(copies, *refs[:13], None, *refs[13:])


def finish_kernel(
    count,
    stride,
    offset,
    all_maps_ref,
    all_values_ref,
    lower_ref,
    upper_ref,
    maps_ref,
    scaled_ref,
    starts_ref,
    out_ref,
    states_ref,
    entry_ref,
):
    me = lax.axis_index("normal")

    def row_map(base):
        return [[all_maps_ref[pl.ds(base + c * COMP + e, 1), :] for e in SIZES] for c in SIZES]

    def row_vector(base):
        return [all_values_ref[pl.ds(base + c, 1), :] for c in SIZES]

    none = (jnp.zeros((1, LANES), jnp.float32),) * COMP

    def forward(device, state):
        for c in SIZES:
            entry_ref[pl.ds(device * PIECES + c, 1), :] = state[c]
        value = row_vector(device * stride + offset)
        return tuple(add(value, times(row_map(device * PADDED), list(state))))

    lax.fori_loop(0, count, forward, none)

    def state_of(device):
        return [entry_ref[pl.ds(device * PIECES + c, 1), :] for c in SIZES]

    def backward(step, state):
        device = count - 1 - step
        value = row_vector(device * stride + offset + COMP)
        value = add(value, times(row_map(device * PADDED + BLOCK), state_of(device)))
        return tuple(add(value, times(row_map(device * PADDED + 2 * BLOCK), list(state))))

    x_in = lax.fori_loop(0, count - 1 - me, backward, none)

    y_in = [jnp.broadcast_to(a, (PIECES, LANES)) for a in state_of(me)]
    x_in = [jnp.broadcast_to(a, (PIECES, LANES)) for a in x_in]

    y_start = add(packed_at(starts_ref, 0), times(map_at(maps_ref, HEAD), y_in))
    x_start = add(packed_at(starts_ref, 1), times(map_at(maps_ref, FROM_Y), y_in))
    x_start = add(x_start, times(map_at(maps_ref, FROM_X), x_in))

    def ahead(step, state):
        state = less(packed_at(scaled_ref, step), times(block_at(lower_ref, step), list(state)))
        put_packed(states_ref, step, state)
        return tuple(state)

    lax.fori_loop(0, STEPS, ahead, tuple(y_start))

    def behind(turn, state):
        step = STEPS - 1 - turn
        state = less(packed_at(states_ref, step), times(block_at(upper_ref, step), list(state)))
        for c in SIZES:
            out_ref[pl.ds(step * COMP + c, PIECES, stride=STEPS * COMP), :] = state[c]
        return tuple(state)

    lax.fori_loop(0, STEPS, behind, tuple(x_start))


def floats(rows):
    return jax.ShapeDtypeStruct((rows, LANES), jnp.float32)


def scratch(rows):
    return pltpu.VMEM((rows, LANES), jnp.float32)


def call(kernel, inputs, out_rows, scratch_rows, name, micros, limit=16 << 20):
    out_shape = [floats(r) for r in out_rows]
    return pl.pallas_call(
        kernel,
        out_shape=out_shape,
        in_specs=[VMEM] * len(inputs),
        out_specs=[VMEM] * len(out_rows),
        scratch_shapes=[scratch(r) for r in scratch_rows],
        compiler_params=pltpu.CompilerParams(vmem_limit_bytes=limit),
        cost_estimate=pl.CostEstimate(
            flops=0, bytes_accessed=int(micros * 3.0e6), transcendentals=0
        ),
        name=name,
    )(*inputs)


def ring(count, step):
    return [(i, (i + step) % count) for i in range(count)]


def per_device(iterate, source, pivot, lower, upper, coupling, iblank, donor):
    count = lax.axis_size("normal")
    x = iterate.reshape(-1, LANES)
    source, pivot, lower, upper, coupling, iblank, donor = (
        a.reshape(-1, LANES) for a in (source, pivot, lower, upper, coupling, iblank, donor)
    )
    field = POINTS * COMP
    state = STEPS * COMP * PIECES

    def around(x):
        return [
            lax.ppermute(x, axis, ring(lax.axis_size(axis), step))
            for axis in ("span", "stream")
            for step in (1, -1)
        ]

    near = around(x)
    maps, whole = call(
        maps_kernel, (lower, upper), (MAPS * BLOCK * PIECES, ROWS), (STEPS * BLOCK * PIECES,), "maps", 2
    )
    (donated,) = call(donate_kernel, (x, donor), (state,), (), "donate", 2)
    fixed = (source, pivot, lower, upper, coupling, iblank)
    sent, scaled, starts = call(
        functools.partial(solve_kernel, 1),
        (x, *near, *fixed, donated, maps, whole),
        (PADDED, state, 2 * COMP * PIECES),
        (state,),
        "solve",
        2,
    )
    everyone = lax.all_gather(sent, "normal", tiled=True)
    (x,) = call(
        functools.partial(finish_kernel, count, PADDED, ROWS),
        (everyone, everyone, lower, upper, maps, scaled, starts),
        (field,),
        (state, count * PIECES),
        "finish",
        2,
    )

    near = around(x)
    (donated,) = call(donate_kernel, (x, donor), (state,), (), "donate", 2)
    sent, scaled, starts = call(
        functools.partial(solve_without, count),
        (x, *near, *fixed, donated, maps),
        (count * VALUES, state, 2 * COMP * PIECES),
        (state,),
        "solve",
        2,
    )
    values = lax.all_to_all(sent.reshape(count, VALUES, 1, LANES), "normal", 0, 0)
    (x,) = call(
        functools.partial(finish_kernel, count, VALUES, 0),
        (everyone, values.reshape(-1, LANES), lower, upper, maps, scaled, starts),
        (field,),
        (state, count * PIECES),
        "finish",
        2,
    )
    return x.reshape(iterate.shape)


def solution(mesh):
    placed = (
        P("normal", None, "span", "stream"),
        P("normal", None, "span", "stream"),
        P("normal", None, None, "span", "stream"),
        P("normal", None, None, "span", "stream"),
        P("normal", None, None, "span", "stream"),
        P(None, "normal", None, None, "span", "stream"),
        P("normal", "span", "stream"),
        P("normal", "span", "stream"),
    )
    return jax.shard_map(
        per_device,
        mesh=mesh,
        in_specs=placed,
        out_specs=P("normal", None, "span", "stream"),
        check_vma=False,
    )
```

```python
import functools

import jax
import jax.numpy as jnp
from jax import lax
from jax.experimental import pallas as pl
from jax.experimental.pallas import tpu as pltpu
from jax.sharding import PartitionSpec as P

COMP = 5
BLOCK = COMP * COMP
PIECES = 8
LANES = 128
STEPS = 6
POINTS = PIECES * STEPS
SIZES = range(COMP)
FWD0, FWD1, FWD2, BWD0, BWD1, BWD2, FOLD, HEAD, FROM_Y, FROM_X = range(10)
MAPS = 10
ROWS = 3 * BLOCK
VALUES = 2 * COMP
PADDED = 88
VMEM = pl.BlockSpec(memory_space=pltpu.VMEM)


def vector_at(ref, step):
    return [ref[pl.ds(step * COMP + c, PIECES, stride=STEPS * COMP), :] for c in SIZES]


def block_at(ref, step, base=0):
    start = base + step * BLOCK
    return [
        [ref[pl.ds(start + c * COMP + e, PIECES, stride=STEPS * BLOCK), :] for e in SIZES]
        for c in SIZES
    ]


def packed_at(ref, step):
    return [ref[pl.ds((step * COMP + c) * PIECES, PIECES), :] for c in SIZES]


def put_packed(ref, step, value):
    for c in SIZES:
        ref[pl.ds((step * COMP + c) * PIECES, PIECES), :] = value[c]


def map_at(ref, which):
    return [
        [ref[pl.ds(((which * COMP + c) * COMP + e) * PIECES, PIECES), :] for e in SIZES]
        for c in SIZES
    ]


def put_map(ref, which, value):
    for c in SIZES:
        for e in SIZES:
            ref[pl.ds(((which * COMP + c) * COMP + e) * PIECES, PIECES), :] = value[c][e]


def total(terms):
    while len(terms) > 1:
        terms = [sum(terms[k : k + 2][1:], terms[k]) for k in range(0, len(terms), 2)]
    return terms[0]


def times(block, vector):
    return [total([block[c][e] * vector[e] for e in SIZES]) for c in SIZES]


def product(left, right):
    return [
        [total([left[c][k] * right[k][e] for k in SIZES]) for e in SIZES] for c in SIZES
    ]


def each(function, *maps):
    return [[function(*(m[c][e] for m in maps)) for e in SIZES] for c in SIZES]


def add(left, right):
    return [a + b for a, b in zip(left, right)]


def less(left, right):
    return [a - b for a, b in zip(left, right)]


def moved(value, steps):
    return pltpu.roll(value, steps % PIECES, 0)


def donate(x_ref, donor_ref, donated_ref):
    lanes, rows = [], []
    for step in range(STEPS):
        place = donor_ref[pl.ds(step, PIECES, stride=STEPS), :]
        lanes.append(place & (LANES - 1))
        rows.append(place >> 7)

    zero = jnp.zeros((PIECES, LANES), jnp.float32)
    for step in range(STEPS):
        found = [zero] * COMP
        for row in range(POINTS):
            here = rows[step] == row
            for c in SIZES:
                line = jnp.broadcast_to(x_ref[pl.ds(row * COMP + c, 1), :], (PIECES, LANES))
                picked = jnp.take_along_axis(line, lanes[step], axis=1, mode="promise_in_bounds")
                found[c] = jnp.where(here, picked, found[c])
        put_packed(donated_ref, step, found)


def donate_kernel(x_ref, donor_ref, donated_ref):
    donate(x_ref, donor_ref, donated_ref)


def start_kernel(*refs):
    given, kept = refs[:8], refs[8:16]
    donated_ref, maps_ref, whole_ref, local_ref, arrived = refs[16:]
    copies = [
        pltpu.make_async_copy(a, b, arrived.at[k]) for k, (a, b) in enumerate(zip(given, kept))
    ]
    for copy in copies:
        copy.start()
    lower_ref, upper_ref, x_ref, donor_ref = kept[:4]
    for copy in copies[:2]:
        copy.wait()
    make_maps(lower_ref, upper_ref, maps_ref, whole_ref, local_ref)
    for copy in copies[2:4]:
        copy.wait()
    donate(x_ref, donor_ref, donated_ref)
    for copy in copies[4:]:
        copy.wait()


def make_maps(lower_ref, upper_ref, maps_ref, whole_ref, local_ref):
    piece = lax.broadcasted_iota(jnp.int32, (PIECES, LANES), 0)
    one = jnp.ones((PIECES, LANES), jnp.float32)
    zero = jnp.zeros((PIECES, LANES), jnp.float32)
    eye = [[one if c == e else zero for e in SIZES] for c in SIZES]

    def pack(value):
        return tuple(value[c][e] for c in SIZES for e in SIZES)

    def unpack(flat):
        return [list(flat[c * COMP : (c + 1) * COMP]) for c in SIZES]

    first = each(lambda a: -a, block_at(lower_ref, 0))
    put_map(local_ref, 0, first)

    def forward(step, state):
        block = block_at(lower_ref, step)
        state = each(lambda a: -a, product(block, unpack(state)))
        put_map(local_ref, step, state)
        return pack(state)

    ahead = unpack(lax.fori_loop(1, STEPS, forward, pack(first)))

    def backward(count, carry):
        behind, fold = unpack(carry[:BLOCK]), unpack(carry[BLOCK:])
        step = STEPS - 1 - count
        block = block_at(upper_ref, step)
        behind = each(lambda a: -a, product(block, behind))
        fold = each(lambda a, b: a - b, map_at(local_ref, step), product(block, fold))
        return pack(behind) + pack(fold)

    last = block_at(upper_ref, STEPS - 1)
    start = pack(each(lambda a: -a, last)) + pack(map_at(local_ref, STEPS - 1))
    carry = lax.fori_loop(1, STEPS, backward, start)
    behind, fold = unpack(carry[:BLOCK]), unpack(carry[BLOCK:])
    put_map(maps_ref, FOLD, fold)

    window = ahead
    for level, shift in enumerate((1, 2, 4)):
        inside = piece >= shift
        put_map(maps_ref, FWD0 + level, each(lambda a: jnp.where(inside, a, 0.0), window))
        longer = product(window, each(lambda a: moved(a, shift), window))
        window = each(lambda a, b: jnp.where(inside, a, b), longer, window)
    head = each(lambda a, b: jnp.where(piece == 0, b, moved(a, 1)), window, eye)
    put_map(maps_ref, HEAD, head)
    for c in SIZES:
        for e in SIZES:
            whole_ref[pl.ds(c * COMP + e, 1), :] = window[c][e][PIECES - 1 :, :]

    window = behind
    response = product(fold, head)
    for level, shift in enumerate((1, 2, 4)):
        inside = piece < PIECES - shift
        masked = each(lambda a: jnp.where(inside, a, 0.0), window)
        put_map(maps_ref, BWD0 + level, masked)
        response = each(
            lambda a, b: a + b,
            response,
            product(masked, each(lambda a: moved(a, -shift), response)),
        )
        longer = product(window, each(lambda a: moved(a, -shift), window))
        window = each(lambda a, b: jnp.where(inside, a, b), longer, window)
    final = piece == PIECES - 1
    put_map(maps_ref, FROM_Y, each(lambda a: jnp.where(final, 0.0, moved(a, -1)), response))
    put_map(maps_ref, FROM_X, each(lambda a, b: jnp.where(final, b, moved(a, -1)), window, eye))
    for c in SIZES:
        for e in SIZES:
            at = c * COMP + e
            whole_ref[pl.ds(BLOCK + at, 1), :] = response[c][e][:1, :]
            whole_ref[pl.ds(2 * BLOCK + at, 1), :] = window[c][e][:1, :]


def solve_kernel(
    copies,
    x_ref,
    below_ref,
    above_ref,
    left_ref,
    right_ref,
    source_ref,
    pivot_ref,
    lower_ref,
    upper_ref,
    coupling_ref,
    iblank_ref,
    donated_ref,
    maps_ref,
    whole_ref,
    sent_ref,
    scaled_ref,
    starts_ref,
    states_ref,
):
    lane = lax.broadcasted_iota(jnp.int32, (PIECES, LANES), 1)
    piece = lax.broadcasted_iota(jnp.int32, (PIECES, LANES), 0)
    zero = jnp.zeros((PIECES, LANES), jnp.float32)

    def forward(step, state):
        x = vector_at(x_ref, step)
        before = [
            pltpu.roll(jnp.where(lane == LANES - 1, a, b), 1, 1)
            for a, b in zip(vector_at(left_ref, step), x)
        ]
        after = [
            pltpu.roll(jnp.where(lane == 0, a, b), LANES - 1, 1)
            for a, b in zip(vector_at(right_ref, step), x)
        ]
        near = [vector_at(below_ref, step), vector_at(above_ref, step), before, after]
        rhs = vector_at(source_ref, step)
        for direc in range(4):
            block = block_at(coupling_ref, step, direc * POINTS * BLOCK)
            for c in SIZES:
                rhs[c] = rhs[c] - total([block[e][c] * near[direc][e] for e in SIZES])
        flag = iblank_ref[pl.ds(step, PIECES, stride=STEPS), :]
        donated = packed_at(donated_ref, step)
        rhs = [
            jnp.where(flag == 0, 0.0, a + jnp.where(flag == 2, b, 0.0))
            for a, b in zip(rhs, donated)
        ]
        scaled = times(block_at(pivot_ref, step), rhs)
        put_packed(scaled_ref, step, scaled)
        state = less(scaled, times(block_at(lower_ref, step), state))
        put_packed(states_ref, step, state)
        return tuple(state)

    ahead = list(lax.fori_loop(0, STEPS, forward, (zero,) * COMP))

    def backward(count, state):
        step = STEPS - 1 - count
        y = packed_at(states_ref, step)
        return tuple(less(y, times(block_at(upper_ref, step), state)))

    behind = list(lax.fori_loop(0, STEPS, backward, (zero,) * COMP))

    for level, shift in enumerate((1, 2, 4)):
        ahead = add(ahead, times(map_at(maps_ref, FWD0 + level), [moved(a, shift) for a in ahead]))
    entry = [jnp.where(piece == 0, 0.0, moved(a, 1)) for a in ahead]
    behind = add(behind, times(map_at(maps_ref, FOLD), entry))
    for level, shift in enumerate((1, 2, 4)):
        behind = add(
            behind, times(map_at(maps_ref, BWD0 + level), [moved(a, -shift) for a in behind])
        )
    put_packed(starts_ref, 0, entry)
    put_packed(
        starts_ref, 1, [jnp.where(piece == PIECES - 1, 0.0, moved(a, -1)) for a in behind]
    )
    if whole_ref is not None:
        sent_ref[pl.ds(0, ROWS), :] = whole_ref[...]
        base = ROWS
        sent_ref[pl.ds(ROWS + VALUES, PADDED - ROWS - VALUES), :] = jnp.zeros(
            (PADDED - ROWS - VALUES, LANES), jnp.float32
        )
    else:
        base = 0
    for copy in range(copies):
        for c in SIZES:
            at = base + copy * VALUES + c
            sent_ref[pl.ds(at, 1), :] = ahead[c][PIECES - 1 :, :]
            sent_ref[pl.ds(at + COMP, 1), :] = behind[c][:1, :]


def solve_without(copies, *refs):
    solve_kernel(copies, *refs[:13], None, *refs[13:])


def finish_kernel(
    count,
    stride,
    offset,
    all_maps_ref,
    all_values_ref,
    lower_ref,
    upper_ref,
    maps_ref,
    scaled_ref,
    starts_ref,
    out_ref,
    states_ref,
    entry_ref,
):
    me = lax.axis_index("normal")

    def row_map(base):
        return [[all_maps_ref[pl.ds(base + c * COMP + e, 1), :] for e in SIZES] for c in SIZES]

    def row_vector(base):
        return [all_values_ref[pl.ds(base + c, 1), :] for c in SIZES]

    none = (jnp.zeros((1, LANES), jnp.float32),) * COMP

    def forward(device, state):
        for c in SIZES:
            entry_ref[pl.ds(device * PIECES + c, 1), :] = state[c]
        value = row_vector(device * stride + offset)
        return tuple(add(value, times(row_map(device * PADDED), list(state))))

    lax.fori_loop(0, count, forward, none)

    def state_of(device):
        return [entry_ref[pl.ds(device * PIECES + c, 1), :] for c in SIZES]

    def backward(step, state):
        device = count - 1 - step
        value = row_vector(device * stride + offset + COMP)
        value = add(value, times(row_map(device * PADDED + BLOCK), state_of(device)))
        return tuple(add(value, times(row_map(device * PADDED + 2 * BLOCK), list(state))))

    x_in = lax.fori_loop(0, count - 1 - me, backward, none)

    y_in = [jnp.broadcast_to(a, (PIECES, LANES)) for a in state_of(me)]
    x_in = [jnp.broadcast_to(a, (PIECES, LANES)) for a in x_in]

    y_start = add(packed_at(starts_ref, 0), times(map_at(maps_ref, HEAD), y_in))
    x_start = add(packed_at(starts_ref, 1), times(map_at(maps_ref, FROM_Y), y_in))
    x_start = add(x_start, times(map_at(maps_ref, FROM_X), x_in))

    def ahead(step, state):
        state = less(packed_at(scaled_ref, step), times(block_at(lower_ref, step), list(state)))
        put_packed(states_ref, step, state)
        return tuple(state)

    lax.fori_loop(0, STEPS, ahead, tuple(y_start))

    def behind(turn, state):
        step = STEPS - 1 - turn
        state = less(packed_at(states_ref, step), times(block_at(upper_ref, step), list(state)))
        for c in SIZES:
            out_ref[pl.ds(step * COMP + c, PIECES, stride=STEPS * COMP), :] = state[c]
        return tuple(state)

    lax.fori_loop(0, STEPS, behind, tuple(x_start))


def floats(rows):
    return jax.ShapeDtypeStruct((rows, LANES), jnp.float32)


def scratch(rows):
    return pltpu.VMEM((rows, LANES), jnp.float32)


def call(kernel, inputs, out_rows, scratch_rows, name, micros, limit=16 << 20):
    out_shape = [floats(r) for r in out_rows]
    return pl.pallas_call(
        kernel,
        out_shape=out_shape,
        in_specs=[VMEM] * len(inputs),
        out_specs=[VMEM] * len(out_rows),
        scratch_shapes=[scratch(r) for r in scratch_rows],
        compiler_params=pltpu.CompilerParams(vmem_limit_bytes=limit),
        cost_estimate=pl.CostEstimate(
            flops=0, bytes_accessed=int(micros * 3.0e6), transcendentals=0
        ),
        name=name,
    )(*inputs)


def ring(count, step):
    return [(i, (i + step) % count) for i in range(count)]


def per_device(iterate, source, pivot, lower, upper, coupling, iblank, donor):
    count = lax.axis_size("normal")
    x = iterate.reshape(-1, LANES)
    source, pivot, lower, upper, coupling, iblank, donor = (
        a.reshape(-1, LANES) for a in (source, pivot, lower, upper, coupling, iblank, donor)
    )
    field = POINTS * COMP
    state = STEPS * COMP * PIECES

    def around(x):
        return [
            lax.ppermute(x, axis, ring(lax.axis_size(axis), step))
            for axis in ("span", "stream")
            for step in (1, -1)
        ]

    near = around(x)
    given = (lower, upper, x, donor, source, pivot, coupling, iblank)
    shapes = [jax.ShapeDtypeStruct(a.shape, a.dtype) for a in given]
    shapes += [floats(r) for r in (state, MAPS * BLOCK * PIECES, ROWS)]
    *given, donated, maps, whole = pl.pallas_call(
        start_kernel,
        out_shape=shapes,
        in_specs=[pl.BlockSpec(memory_space=pltpu.HBM)] * len(given),
        out_specs=[VMEM] * len(shapes),
        scratch_shapes=[scratch(STEPS * BLOCK * PIECES), pltpu.SemaphoreType.DMA((len(given),))],
        compiler_params=pltpu.CompilerParams(vmem_limit_bytes=16 << 20),
        cost_estimate=pl.CostEstimate(flops=0, bytes_accessed=12 << 20, transcendentals=0),
        name="start",
    )(*(pltpu.with_memory_space_constraint(a, pltpu.HBM) for a in given))
    lower, upper, x, donor, source, pivot, coupling, iblank = given
    fixed = (source, pivot, lower, upper, coupling, iblank)
    sent, scaled, starts = call(
        functools.partial(solve_kernel, 1),
        (x, *near, *fixed, donated, maps, whole),
        (PADDED, state, 2 * COMP * PIECES),
        (state,),
        "solve",
        2,
    )
    everyone = lax.all_gather(sent, "normal", tiled=True)
    (x,) = call(
        functools.partial(finish_kernel, count, PADDED, ROWS),
        (everyone, everyone, lower, upper, maps, scaled, starts),
        (field,),
        (state, count * PIECES),
        "finish",
        2,
    )

    near = around(x)
    (donated,) = call(donate_kernel, (x, donor), (state,), (), "donate", 2)
    sent, scaled, starts = call(
        functools.partial(solve_without, count),
        (x, *near, *fixed, donated, maps),
        (count * VALUES, state, 2 * COMP * PIECES),
        (state,),
        "solve",
        2,
    )
    values = lax.all_to_all(sent.reshape(count, VALUES, 1, LANES), "normal", 0, 0)
    (x,) = call(
        functools.partial(finish_kernel, count, VALUES, 0),
        (everyone, values.reshape(-1, LANES), lower, upper, maps, scaled, starts),
        (field,),
        (state, count * PIECES),
        "finish",
        2,
    )
    return x.reshape(iterate.shape)


def solution(mesh):
    placed = (
        P("normal", None, "span", "stream"),
        P("normal", None, "span", "stream"),
        P("normal", None, None, "span", "stream"),
        P("normal", None, None, "span", "stream"),
        P("normal", None, None, "span", "stream"),
        P(None, "normal", None, None, "span", "stream"),
        P("normal", "span", "stream"),
        P("normal", "span", "stream"),
    )
    return jax.shard_map(
        per_device,
        mesh=mesh,
        in_specs=placed,
        out_specs=P("normal", None, "span", "stream"),
        check_vma=False,
    )
```

```python
import functools

import jax
import jax.numpy as jnp
from jax import lax
from jax.experimental import pallas as pl
from jax.experimental.pallas import tpu as pltpu
from jax.sharding import PartitionSpec as P

COMP = 5
BLOCK = COMP * COMP
PIECES = 8
LANES = 128
STEPS = 6
POINTS = PIECES * STEPS
SIZES = range(COMP)
FWD0, FWD1, FWD2, BWD0, BWD1, BWD2, FOLD, HEAD, FROM_Y, FROM_X = range(10)
MAPS = 10
ROWS = 3 * BLOCK
VALUES = 2 * COMP
MEMBERS = 4
PADDED = 76
SHARE = PADDED // MEMBERS
SLOT = VALUES + SHARE
VMEM = pl.BlockSpec(memory_space=pltpu.VMEM)


def vector_at(ref, step):
    return [ref[pl.ds(step * COMP + c, PIECES, stride=STEPS * COMP), :] for c in SIZES]


def block_at(ref, step, base=0):
    start = base + step * BLOCK
    return [
        [ref[pl.ds(start + c * COMP + e, PIECES, stride=STEPS * BLOCK), :] for e in SIZES]
        for c in SIZES
    ]


def packed_at(ref, step):
    return [ref[pl.ds((step * COMP + c) * PIECES, PIECES), :] for c in SIZES]


def put_packed(ref, step, value):
    for c in SIZES:
        ref[pl.ds((step * COMP + c) * PIECES, PIECES), :] = value[c]


def map_at(ref, which):
    return [
        [ref[pl.ds(((which * COMP + c) * COMP + e) * PIECES, PIECES), :] for e in SIZES]
        for c in SIZES
    ]


def put_map(ref, which, value):
    for c in SIZES:
        for e in SIZES:
            ref[pl.ds(((which * COMP + c) * COMP + e) * PIECES, PIECES), :] = value[c][e]


def total(terms):
    while len(terms) > 1:
        terms = [sum(terms[k : k + 2][1:], terms[k]) for k in range(0, len(terms), 2)]
    return terms[0]


def times(block, vector):
    return [total([block[c][e] * vector[e] for e in SIZES]) for c in SIZES]


def product(left, right):
    return [
        [total([left[c][k] * right[k][e] for k in SIZES]) for e in SIZES] for c in SIZES
    ]


def each(function, *maps):
    return [[function(*(m[c][e] for m in maps)) for e in SIZES] for c in SIZES]


def add(left, right):
    return [a + b for a, b in zip(left, right)]


def less(left, right):
    return [a - b for a, b in zip(left, right)]


def moved(value, steps):
    return pltpu.roll(value, steps % PIECES, 0)


def donate(x_ref, donor_ref, donated_ref):
    lanes, rows = [], []
    for step in range(STEPS):
        place = donor_ref[pl.ds(step, PIECES, stride=STEPS), :]
        lanes.append(place & (LANES - 1))
        rows.append(place >> 7)

    zero = jnp.zeros((PIECES, LANES), jnp.float32)
    for step in range(STEPS):
        found = [zero] * COMP
        for row in range(POINTS):
            here = rows[step] == row
            for c in SIZES:
                line = jnp.broadcast_to(x_ref[pl.ds(row * COMP + c, 1), :], (PIECES, LANES))
                picked = jnp.take_along_axis(line, lanes[step], axis=1, mode="promise_in_bounds")
                found[c] = jnp.where(here, picked, found[c])
        put_packed(donated_ref, step, found)


def donate_kernel(x_ref, donor_ref, donated_ref):
    donate(x_ref, donor_ref, donated_ref)


def summary_kernel(lower_in, upper_in, whole_out, lower_ref, upper_ref, maps_ref, whole_ref, local_ref, moves):
    copies = [
        pltpu.make_async_copy(a, b, moves.at[k])
        for k, (a, b) in enumerate(((lower_in, lower_ref), (upper_in, upper_ref)))
    ]
    for copy in copies:
        copy.start()
    for copy in copies:
        copy.wait()
    make_maps(lower_ref, upper_ref, maps_ref, whole_ref, local_ref)
    copy = pltpu.make_async_copy(whole_ref, whole_out, moves.at[2])
    copy.start()
    copy.wait()


def start_kernel(*refs):
    members_ref, given, kept = refs[0], refs[1:9], refs[9:17]
    donated_ref, maps_ref, share_ref, outer_ref = refs[17:21]
    whole_ref, local_ref, group_ref, work_ref, arrived = refs[21:]
    copies = [
        pltpu.make_async_copy(a, b, arrived.at[k]) for k, (a, b) in enumerate(zip(given, kept))
    ]
    for copy in copies:
        copy.start()
    lower_ref, upper_ref, x_ref, donor_ref = kept[:4]
    for copy in copies[:2]:
        copy.wait()
    make_maps(lower_ref, upper_ref, maps_ref, whole_ref, local_ref)
    group_maps(members_ref, share_ref, outer_ref, group_ref, work_ref)
    for copy in copies[2:4]:
        copy.wait()
    donate(x_ref, donor_ref, donated_ref)
    for copy in copies[4:]:
        copy.wait()


def put_whole(ref, at, row):
    for member in range(MEMBERS):
        ref[pl.ds(member * PADDED + at, 1), :] = row


def make_maps(lower_ref, upper_ref, maps_ref, whole_ref, local_ref):
    piece = lax.broadcasted_iota(jnp.int32, (PIECES, LANES), 0)
    one = jnp.ones((PIECES, LANES), jnp.float32)
    zero = jnp.zeros((PIECES, LANES), jnp.float32)
    eye = [[one if c == e else zero for e in SIZES] for c in SIZES]

    def pack(value):
        return tuple(value[c][e] for c in SIZES for e in SIZES)

    def unpack(flat):
        return [list(flat[c * COMP : (c + 1) * COMP]) for c in SIZES]

    first = each(lambda a: -a, block_at(lower_ref, 0))
    put_map(local_ref, 0, first)

    def forward(step, state):
        block = block_at(lower_ref, step)
        state = each(lambda a: -a, product(block, unpack(state)))
        put_map(local_ref, step, state)
        return pack(state)

    ahead = unpack(lax.fori_loop(1, STEPS, forward, pack(first)))

    def backward(count, carry):
        behind, fold = unpack(carry[:BLOCK]), unpack(carry[BLOCK:])
        step = STEPS - 1 - count
        block = block_at(upper_ref, step)
        behind = each(lambda a: -a, product(block, behind))
        fold = each(lambda a, b: a - b, map_at(local_ref, step), product(block, fold))
        return pack(behind) + pack(fold)

    last = block_at(upper_ref, STEPS - 1)
    start = pack(each(lambda a: -a, last)) + pack(map_at(local_ref, STEPS - 1))
    carry = lax.fori_loop(1, STEPS, backward, start)
    behind, fold = unpack(carry[:BLOCK]), unpack(carry[BLOCK:])
    put_map(maps_ref, FOLD, fold)

    window = ahead
    for level, shift in enumerate((1, 2, 4)):
        inside = piece >= shift
        put_map(maps_ref, FWD0 + level, each(lambda a: jnp.where(inside, a, 0.0), window))
        longer = product(window, each(lambda a: moved(a, shift), window))
        window = each(lambda a, b: jnp.where(inside, a, b), longer, window)
    head = each(lambda a, b: jnp.where(piece == 0, b, moved(a, 1)), window, eye)
    put_map(maps_ref, HEAD, head)
    for c in SIZES:
        for e in SIZES:
            put_whole(whole_ref, c * COMP + e, window[c][e][PIECES - 1 :, :])

    window = behind
    response = product(fold, head)
    for level, shift in enumerate((1, 2, 4)):
        inside = piece < PIECES - shift
        masked = each(lambda a: jnp.where(inside, a, 0.0), window)
        put_map(maps_ref, BWD0 + level, masked)
        response = each(
            lambda a, b: a + b,
            response,
            product(masked, each(lambda a: moved(a, -shift), response)),
        )
        longer = product(window, each(lambda a: moved(a, -shift), window))
        window = each(lambda a, b: jnp.where(inside, a, b), longer, window)
    final = piece == PIECES - 1
    put_map(maps_ref, FROM_Y, each(lambda a: jnp.where(final, 0.0, moved(a, -1)), response))
    put_map(maps_ref, FROM_X, each(lambda a, b: jnp.where(final, b, moved(a, -1)), window, eye))
    for c in SIZES:
        for e in SIZES:
            at = c * COMP + e
            put_whole(whole_ref, BLOCK + at, response[c][e][:1, :])
            put_whole(whole_ref, 2 * BLOCK + at, window[c][e][:1, :])
    put_whole(whole_ref, ROWS, jnp.zeros((1, LANES), jnp.float32))


def solve_kernel(
    count,
    x_ref,
    below_ref,
    above_ref,
    left_ref,
    right_ref,
    source_ref,
    pivot_ref,
    lower_ref,
    upper_ref,
    coupling_ref,
    iblank_ref,
    donated_ref,
    maps_ref,
    outer_ref,
    share_ref,
    sent_ref,
    scaled_ref,
    starts_ref,
    states_ref,
):
    lane = lax.broadcasted_iota(jnp.int32, (PIECES, LANES), 1)
    piece = lax.broadcasted_iota(jnp.int32, (PIECES, LANES), 0)
    zero = jnp.zeros((PIECES, LANES), jnp.float32)

    def forward(step, state):
        x = vector_at(x_ref, step)
        before = [
            pltpu.roll(jnp.where(lane == LANES - 1, a, b), 1, 1)
            for a, b in zip(vector_at(left_ref, step), x)
        ]
        after = [
            pltpu.roll(jnp.where(lane == 0, a, b), LANES - 1, 1)
            for a, b in zip(vector_at(right_ref, step), x)
        ]
        near = [vector_at(below_ref, step), vector_at(above_ref, step), before, after]
        rhs = vector_at(source_ref, step)
        for direc in range(4):
            block = block_at(coupling_ref, step, direc * POINTS * BLOCK)
            for c in SIZES:
                rhs[c] = rhs[c] - total([block[e][c] * near[direc][e] for e in SIZES])
        flag = iblank_ref[pl.ds(step, PIECES, stride=STEPS), :]
        donated = packed_at(donated_ref, step)
        rhs = [
            jnp.where(flag == 0, 0.0, a + jnp.where(flag == 2, b, 0.0))
            for a, b in zip(rhs, donated)
        ]
        scaled = times(block_at(pivot_ref, step), rhs)
        put_packed(scaled_ref, step, scaled)
        state = less(scaled, times(block_at(lower_ref, step), state))
        put_packed(states_ref, step, state)
        return tuple(state)

    ahead = list(lax.fori_loop(0, STEPS, forward, (zero,) * COMP))

    def backward(count, state):
        step = STEPS - 1 - count
        y = packed_at(states_ref, step)
        return tuple(less(y, times(block_at(upper_ref, step), state)))

    behind = list(lax.fori_loop(0, STEPS, backward, (zero,) * COMP))

    for level, shift in enumerate((1, 2, 4)):
        ahead = add(ahead, times(map_at(maps_ref, FWD0 + level), [moved(a, shift) for a in ahead]))
    entry = [jnp.where(piece == 0, 0.0, moved(a, 1)) for a in ahead]
    behind = add(behind, times(map_at(maps_ref, FOLD), entry))
    for level, shift in enumerate((1, 2, 4)):
        behind = add(
            behind, times(map_at(maps_ref, BWD0 + level), [moved(a, -shift) for a in behind])
        )
    put_packed(starts_ref, 0, entry)
    put_packed(
        starts_ref, 1, [jnp.where(piece == PIECES - 1, 0.0, moved(a, -1)) for a in behind]
    )
    y_out = [jnp.broadcast_to(a[PIECES - 1 :, :], (COMP, LANES)) for a in ahead]
    x_out = [jnp.broadcast_to(a[:1, :], (COMP, LANES)) for a in behind]
    row = lax.broadcasted_iota(jnp.int32, (COMP, LANES), 0)

    def stacked(rows):
        out = rows[0]
        for c in SIZES[1:]:
            out = jnp.where(row == c, rows[c], out)
        return out

    def outer(which, rows):
        return total([outer_ref[pl.ds((which * COMP + e) * PIECES, COMP), :] * rows[e] for e in SIZES])

    inside = stacked(y_out), stacked(x_out)
    outside = outer(0, y_out), outer(1, y_out) + outer(2, x_out)
    mine = lax.axis_index("normal") // MEMBERS
    slot = VALUES if share_ref is None else SLOT
    for device in range(count):
        same = mine == device // MEMBERS
        for k in range(2):
            at = device * slot + k * COMP
            sent_ref[pl.ds(at, COMP), :] = jnp.where(same, inside[k], outside[k])
        if share_ref is not None:
            sent_ref[pl.ds(device * slot + VALUES, SHARE), :] = share_ref[pl.ds(0, SHARE), :]


def solve_without(count, *refs):
    solve_kernel(count, *refs[:14], None, *refs[14:])


def group_maps(members_ref, share_ref, outer_ref, whole_ref, work_ref):
    own = lax.rem(lax.axis_index("normal"), MEMBERS)
    row = lax.broadcasted_iota(jnp.int32, (COMP, LANES), 0)
    eye = [jnp.where(row == e, 1.0, 0.0) for e in SIZES]
    none = [jnp.zeros((COMP, LANES), jnp.float32)] * COMP

    def given(member, which):
        base = member * PADDED + which * BLOCK
        columns = [members_ref[pl.ds(base + e, COMP, stride=COMP), :] for e in SIZES]
        return columns, lambda k, e: members_ref[pl.ds(base + k * COMP + e, 1), :]

    def kept(columns, place):
        for e in SIZES:
            work_ref[pl.ds((place * COMP + e) * PIECES, COMP), :] = columns[e]
        return lambda k, e: work_ref[pl.ds((place * COMP + e) * PIECES + k, 1), :]

    def multiply(columns, element):
        return [total([columns[k] * element(k, e) for k in SIZES]) for e in SIZES]

    def chosen(options):
        out = options[-1]
        for member in range(MEMBERS - 1):
            out = [jnp.where(own == member, a, b) for a, b in zip(options[member], out)]
        return out

    onward, across = [given(MEMBERS - 1, 0)[0]], [given(MEMBERS - 1, 1)[0]]
    for member in range(MEMBERS - 2, -1, -1):
        forward = given(member, 0)[1]
        onward.insert(0, multiply(onward[0], forward))
        inner = kept(multiply(across[0], forward), member)
        across.insert(0, add(given(member, 1)[0], multiply(given(member, 2)[0], inner)))
    back = [eye, given(0, 2)[0]]
    for member in range(1, MEMBERS):
        back.append(multiply(back[-1], given(member, 2)[1]))
    mixed = multiply(
        chosen(back[1:MEMBERS] + [none]), kept(chosen(across[1:] + [none]), MEMBERS - 1)
    )
    for k, columns in enumerate((chosen(onward[1:] + [eye]), mixed, chosen(back[:MEMBERS]))):
        for e in SIZES:
            outer_ref[pl.ds((k * COMP + e) * PIECES, COMP), :] = columns[e]
    for k, columns in enumerate((onward[0], across[0], back[MEMBERS])):
        for e in SIZES:
            whole_ref[pl.ds(k * BLOCK + e, COMP, stride=COMP), :] = columns[e]
    whole_ref[pl.ds(ROWS, 1), :] = jnp.zeros((1, LANES), jnp.float32)
    share_ref[pl.ds(0, SHARE), :] = whole_ref[pl.ds(own * SHARE, SHARE), :]


def finish_kernel(
    count,
    slot,
    values_ref,
    shares_ref,
    members_ref,
    lower_ref,
    upper_ref,
    maps_ref,
    scaled_ref,
    starts_ref,
    out_ref,
    states_ref,
    entry_ref,
):
    me = lax.axis_index("normal")
    mine, own = me // MEMBERS, lax.rem(me, MEMBERS)
    groups = count // MEMBERS

    def group_map(group, which):
        def row(at):
            place = (group * MEMBERS + at // SHARE) * SLOT + VALUES + at % SHARE
            return shares_ref[pl.ds(place, 1), :]

        return [[row((which * COMP + c) * COMP + e) for e in SIZES] for c in SIZES]

    def member_map(member, which):
        base = member * PADDED + which * BLOCK
        return [[members_ref[pl.ds(base + c * COMP + e, 1), :] for e in SIZES] for c in SIZES]

    def value(device, which):
        return [values_ref[pl.ds(device * slot + which * COMP + c, 1), :] for c in SIZES]

    def group_value(group, which):
        parts = [value(group * MEMBERS + member, which) for member in range(MEMBERS)]
        return [total([part[c] for part in parts]) for c in SIZES]

    def put_entry(at, state):
        for c in SIZES:
            entry_ref[pl.ds(at * PIECES + c, 1), :] = state[c]

    def entry(at):
        return [entry_ref[pl.ds(at * PIECES + c, 1), :] for c in SIZES]

    none = (jnp.zeros((1, LANES), jnp.float32),) * COMP

    def over_group(group, state):
        put_entry(group, state)
        return tuple(add(group_value(group, 0), times(group_map(group, 0), list(state))))

    state = lax.fori_loop(0, mine, over_group, none)
    for member in range(MEMBERS):
        put_entry(groups + member, state)
        state = add(value(mine * MEMBERS + member, 0), times(member_map(member, 0), list(state)))
    lax.fori_loop(mine + 1, groups, over_group, tuple(state))

    def back_over_group(step, state):
        group = groups - 1 - step
        inner = add(group_value(group, 1), times(group_map(group, 1), entry(group)))
        return tuple(add(inner, times(group_map(group, 2), list(state))))

    state = lax.fori_loop(0, groups - 1 - mine, back_over_group, none)

    def back_over_member(step, state):
        member = MEMBERS - 1 - step
        inner = add(
            value(mine * MEMBERS + member, 1), times(member_map(member, 1), entry(groups + member))
        )
        return tuple(add(inner, times(member_map(member, 2), list(state))))

    x_in = lax.fori_loop(0, MEMBERS - 1 - own, back_over_member, state)

    y_in = [jnp.broadcast_to(a, (PIECES, LANES)) for a in entry(groups + own)]
    x_in = [jnp.broadcast_to(a, (PIECES, LANES)) for a in x_in]

    y_start = add(packed_at(starts_ref, 0), times(map_at(maps_ref, HEAD), y_in))
    x_start = add(packed_at(starts_ref, 1), times(map_at(maps_ref, FROM_Y), y_in))
    x_start = add(x_start, times(map_at(maps_ref, FROM_X), x_in))

    def ahead(step, state):
        state = less(packed_at(scaled_ref, step), times(block_at(lower_ref, step), list(state)))
        put_packed(states_ref, step, state)
        return tuple(state)

    lax.fori_loop(0, STEPS, ahead, tuple(y_start))

    def behind(turn, state):
        step = STEPS - 1 - turn
        state = less(packed_at(states_ref, step), times(block_at(upper_ref, step), list(state)))
        for c in SIZES:
            out_ref[pl.ds(step * COMP + c, PIECES, stride=STEPS * COMP), :] = state[c]
        return tuple(state)

    lax.fori_loop(0, STEPS, behind, tuple(x_start))


def floats(rows):
    return jax.ShapeDtypeStruct((rows, LANES), jnp.float32)


def scratch(rows):
    return pltpu.VMEM((rows, LANES), jnp.float32)


def call(kernel, inputs, outputs, scratches, name, micros, far=()):
    hbm = pl.BlockSpec(memory_space=pltpu.HBM)
    places = range(len(inputs) + len(outputs))
    specs = [hbm if k in far else VMEM for k in places]
    inputs = [
        pltpu.with_memory_space_constraint(a, pltpu.HBM) if k in far else a
        for k, a in enumerate(inputs)
    ]
    return pl.pallas_call(
        kernel,
        out_shape=[floats(a) if isinstance(a, int) else a for a in outputs],
        in_specs=specs[: len(inputs)],
        out_specs=specs[len(inputs) :],
        scratch_shapes=[scratch(a) if isinstance(a, int) else a for a in scratches],
        compiler_params=pltpu.CompilerParams(vmem_limit_bytes=16 << 20),
        cost_estimate=pl.CostEstimate(
            flops=0, bytes_accessed=int(micros * 3.0e6), transcendentals=0
        ),
        name=name,
    )(*inputs)


def ring(count, step):
    return [(i, (i + step) % count) for i in range(count)]


def per_device(iterate, source, pivot, lower, upper, coupling, iblank, donor):
    count = lax.axis_size("normal")
    x = iterate.reshape(-1, LANES)
    source, pivot, lower, upper, coupling, iblank, donor = (
        a.reshape(-1, LANES) for a in (source, pivot, lower, upper, coupling, iblank, donor)
    )
    field = POINTS * COMP
    state = STEPS * COMP * PIECES

    def around(x):
        return [
            lax.ppermute(x, axis, ring(lax.axis_size(axis), step))
            for axis in ("span", "stream")
            for step in (1, -1)
        ]

    def exchanged(rows, parts, groups=None):
        rows = rows.reshape(parts, -1, 1, LANES)
        return lax.all_to_all(rows, "normal", 0, 0, axis_index_groups=groups).reshape(-1, LANES)

    maps_rows = MAPS * BLOCK * PIECES
    local_rows = STEPS * BLOCK * PIECES
    whole_rows = MEMBERS * PADDED
    entries = (count // MEMBERS + MEMBERS) * PIECES

    (whole,) = call(
        summary_kernel,
        (lower, upper),
        (whole_rows,),
        (
            lower.shape[0],
            upper.shape[0],
            maps_rows,
            whole_rows,
            local_rows,
            pltpu.SemaphoreType.DMA((3,)),
        ),
        "summary",
        2,
        far=(0, 1, 2),
    )
    groups = [list(range(k, k + MEMBERS)) for k in range(0, count, MEMBERS)]
    members = exchanged(whole, MEMBERS, groups)
    near = around(x)
    given = (lower, upper, x, donor, source, pivot, coupling, iblank)
    *given, donated, maps, share, outer = call(
        start_kernel,
        (members, *given),
        [jax.ShapeDtypeStruct(a.shape, a.dtype) for a in given]
        + [state, maps_rows, 24, 3 * COMP * PIECES],
        (
            whole_rows,
            local_rows,
            PADDED + 4,
            MEMBERS * COMP * PIECES,
            pltpu.SemaphoreType.DMA((len(given),)),
        ),
        "start",
        4,
        far=range(1, len(given) + 1),
    )
    lower, upper, x, donor, source, pivot, coupling, iblank = given
    fixed = (source, pivot, lower, upper, coupling, iblank)
    sent, scaled, starts = call(
        functools.partial(solve_kernel, count),
        (x, *near, *fixed, donated, maps, outer, share),
        (count * SLOT, state, 2 * COMP * PIECES),
        (state,),
        "solve",
        2,
    )
    shares = exchanged(sent, count)
    (x,) = call(
        functools.partial(finish_kernel, count, SLOT),
        (shares, shares, members, lower, upper, maps, scaled, starts),
        (field,),
        (state, entries),
        "finish",
        1,
    )

    near = around(x)
    (donated,) = call(donate_kernel, (x, donor), (state,), (), "donate", 2)
    sent, scaled, starts = call(
        functools.partial(solve_without, count),
        (x, *near, *fixed, donated, maps, outer),
        (count * VALUES, state, 2 * COMP * PIECES),
        (state,),
        "solve",
        2,
    )
    values = exchanged(sent, count)
    (x,) = call(
        functools.partial(finish_kernel, count, VALUES),
        (values, shares, members, lower, upper, maps, scaled, starts),
        (field,),
        (state, entries),
        "finish",
        1,
    )
    return x.reshape(iterate.shape)


def solution(mesh):
    placed = (
        P("normal", None, "span", "stream"),
        P("normal", None, "span", "stream"),
        P("normal", None, None, "span", "stream"),
        P("normal", None, None, "span", "stream"),
        P("normal", None, None, "span", "stream"),
        P(None, "normal", None, None, "span", "stream"),
        P("normal", "span", "stream"),
        P("normal", "span", "stream"),
    )
    return jax.shard_map(
        per_device,
        mesh=mesh,
        in_specs=placed,
        out_specs=P("normal", None, "span", "stream"),
        check_vma=False,
    )
```

```python
import functools

import jax
import jax.numpy as jnp
from jax import lax
from jax.experimental import pallas as pl
from jax.experimental.pallas import tpu as pltpu
from jax.sharding import PartitionSpec as P

COMP = 5
BLOCK = COMP * COMP
PIECES = 8
LANES = 128
STEPS = 6
POINTS = PIECES * STEPS
SIZES = range(COMP)
FWD0, FWD1, FWD2, BWD0, BWD1, BWD2, FOLD, HEAD, FROM_Y, FROM_X = range(10)
MAPS = 10
ROWS = 3 * BLOCK
VALUES = 2 * COMP
MEMBERS = 4
PADDED = 76
SHARE = PADDED // MEMBERS
SLOT = VALUES + SHARE
VMEM = pl.BlockSpec(memory_space=pltpu.VMEM)


def vector_at(ref, step):
    return [ref[pl.ds(step * COMP + c, PIECES, stride=STEPS * COMP), :] for c in SIZES]


def block_at(ref, step, base=0):
    start = base + step * BLOCK
    return [
        [ref[pl.ds(start + c * COMP + e, PIECES, stride=STEPS * BLOCK), :] for e in SIZES]
        for c in SIZES
    ]


def packed_at(ref, step):
    return [ref[pl.ds((step * COMP + c) * PIECES, PIECES), :] for c in SIZES]


def put_packed(ref, step, value):
    for c in SIZES:
        ref[pl.ds((step * COMP + c) * PIECES, PIECES), :] = value[c]


def map_at(ref, which):
    return [
        [ref[pl.ds(((which * COMP + c) * COMP + e) * PIECES, PIECES), :] for e in SIZES]
        for c in SIZES
    ]


def put_map(ref, which, value):
    for c in SIZES:
        for e in SIZES:
            ref[pl.ds(((which * COMP + c) * COMP + e) * PIECES, PIECES), :] = value[c][e]


def total(terms):
    while len(terms) > 1:
        terms = [sum(terms[k : k + 2][1:], terms[k]) for k in range(0, len(terms), 2)]
    return terms[0]


def times(block, vector):
    return [total([block[c][e] * vector[e] for e in SIZES]) for c in SIZES]


def product(left, right):
    return [
        [total([left[c][k] * right[k][e] for k in SIZES]) for e in SIZES] for c in SIZES
    ]


def each(function, *maps):
    return [[function(*(m[c][e] for m in maps)) for e in SIZES] for c in SIZES]


def add(left, right):
    return [a + b for a, b in zip(left, right)]


def less(left, right):
    return [a - b for a, b in zip(left, right)]


def moved(value, steps):
    return pltpu.roll(value, steps % PIECES, 0)


def donate(x_ref, donor_ref, donated_ref):
    lanes, rows = [], []
    for step in range(STEPS):
        place = donor_ref[pl.ds(step, PIECES, stride=STEPS), :]
        lanes.append(place & (LANES - 1))
        rows.append(place >> 7)

    zero = jnp.zeros((PIECES, LANES), jnp.float32)
    for step in range(STEPS):
        found = [zero] * COMP
        for row in range(POINTS):
            here = rows[step] == row
            for c in SIZES:
                line = jnp.broadcast_to(x_ref[pl.ds(row * COMP + c, 1), :], (PIECES, LANES))
                picked = jnp.take_along_axis(line, lanes[step], axis=1, mode="promise_in_bounds")
                found[c] = jnp.where(here, picked, found[c])
        put_packed(donated_ref, step, found)


def donate_kernel(x_ref, donor_ref, donated_ref):
    donate(x_ref, donor_ref, donated_ref)


def no_edges():
    return (jnp.zeros((PIECES, LANES), jnp.float32),) * 2


def with_edges(vector, step, first, last):
    lane = lax.broadcasted_iota(jnp.int32, (PIECES, LANES), 1)
    for c in SIZES:
        here = lane == step * COMP + c
        first = jnp.where(here, jnp.broadcast_to(vector[c][:, :1], (PIECES, LANES)), first)
        last = jnp.where(here, jnp.broadcast_to(vector[c][:, -1:], (PIECES, LANES)), last)
    return first, last


def summary_kernel(lower_in, upper_in, whole_out, lower_ref, upper_ref, maps_ref, whole_ref, local_ref, moves):
    copies = [
        pltpu.make_async_copy(a, b, moves.at[k])
        for k, (a, b) in enumerate(((lower_in, lower_ref), (upper_in, upper_ref)))
    ]
    for copy in copies:
        copy.start()
    for copy in copies:
        copy.wait()
    make_maps(lower_ref, upper_ref, maps_ref, whole_ref, local_ref)
    copy = pltpu.make_async_copy(whole_ref, whole_out, moves.at[2])
    copy.start()
    copy.wait()


def start_kernel(*refs):
    members_ref, given, kept = refs[0], refs[1:9], refs[9:17]
    donated_ref, maps_ref, share_ref, outer_ref = refs[17:21]
    whole_ref, local_ref, group_ref, work_ref, arrived = refs[21:]
    copies = [
        pltpu.make_async_copy(a, b, arrived.at[k]) for k, (a, b) in enumerate(zip(given, kept))
    ]
    for copy in copies:
        copy.start()
    lower_ref, upper_ref, x_ref, donor_ref = kept[:4]
    group_maps(members_ref, share_ref, outer_ref, group_ref, work_ref)
    for copy in copies[:2]:
        copy.wait()
    make_maps(lower_ref, upper_ref, maps_ref, whole_ref, local_ref)
    for copy in copies[2:4]:
        copy.wait()
    donate(x_ref, donor_ref, donated_ref)
    for copy in copies[4:]:
        copy.wait()


def put_whole(ref, at, row):
    for member in range(MEMBERS):
        ref[pl.ds(member * PADDED + at, 1), :] = row


def make_maps(lower_ref, upper_ref, maps_ref, whole_ref, local_ref):
    piece = lax.broadcasted_iota(jnp.int32, (PIECES, LANES), 0)
    one = jnp.ones((PIECES, LANES), jnp.float32)
    zero = jnp.zeros((PIECES, LANES), jnp.float32)
    eye = [[one if c == e else zero for e in SIZES] for c in SIZES]

    def pack(value):
        return tuple(value[c][e] for c in SIZES for e in SIZES)

    def unpack(flat):
        return [list(flat[c * COMP : (c + 1) * COMP]) for c in SIZES]

    first = each(lambda a: -a, block_at(lower_ref, 0))
    put_map(local_ref, 0, first)

    def forward(step, state):
        block = block_at(lower_ref, step)
        state = each(lambda a: -a, product(block, unpack(state)))
        put_map(local_ref, step, state)
        return pack(state)

    ahead = unpack(lax.fori_loop(1, STEPS, forward, pack(first)))

    def backward(count, carry):
        behind, fold = unpack(carry[:BLOCK]), unpack(carry[BLOCK:])
        step = STEPS - 1 - count
        block = block_at(upper_ref, step)
        behind = each(lambda a: -a, product(block, behind))
        fold = each(lambda a, b: a - b, map_at(local_ref, step), product(block, fold))
        return pack(behind) + pack(fold)

    last = block_at(upper_ref, STEPS - 1)
    start = pack(each(lambda a: -a, last)) + pack(map_at(local_ref, STEPS - 1))
    carry = lax.fori_loop(1, STEPS, backward, start)
    behind, fold = unpack(carry[:BLOCK]), unpack(carry[BLOCK:])
    put_map(maps_ref, FOLD, fold)

    window = ahead
    for level, shift in enumerate((1, 2, 4)):
        inside = piece >= shift
        put_map(maps_ref, FWD0 + level, each(lambda a: jnp.where(inside, a, 0.0), window))
        longer = product(window, each(lambda a: moved(a, shift), window))
        window = each(lambda a, b: jnp.where(inside, a, b), longer, window)
    head = each(lambda a, b: jnp.where(piece == 0, b, moved(a, 1)), window, eye)
    put_map(maps_ref, HEAD, head)
    for c in SIZES:
        for e in SIZES:
            put_whole(whole_ref, c * COMP + e, window[c][e][PIECES - 1 :, :])

    window = behind
    response = product(fold, head)
    for level, shift in enumerate((1, 2, 4)):
        inside = piece < PIECES - shift
        masked = each(lambda a: jnp.where(inside, a, 0.0), window)
        put_map(maps_ref, BWD0 + level, masked)
        response = each(
            lambda a, b: a + b,
            response,
            product(masked, each(lambda a: moved(a, -shift), response)),
        )
        longer = product(window, each(lambda a: moved(a, -shift), window))
        window = each(lambda a, b: jnp.where(inside, a, b), longer, window)
    final = piece == PIECES - 1
    put_map(maps_ref, FROM_Y, each(lambda a: jnp.where(final, 0.0, moved(a, -1)), response))
    put_map(maps_ref, FROM_X, each(lambda a, b: jnp.where(final, b, moved(a, -1)), window, eye))
    for c in SIZES:
        for e in SIZES:
            at = c * COMP + e
            put_whole(whole_ref, BLOCK + at, response[c][e][:1, :])
            put_whole(whole_ref, 2 * BLOCK + at, window[c][e][:1, :])
    put_whole(whole_ref, ROWS, jnp.zeros((1, LANES), jnp.float32))


def solve_kernel(
    count,
    x_ref,
    below_ref,
    above_ref,
    left_ref,
    right_ref,
    source_ref,
    pivot_ref,
    lower_ref,
    upper_ref,
    coupling_ref,
    iblank_ref,
    donated_ref,
    maps_ref,
    outer_ref,
    share_ref,
    sent_ref,
    scaled_ref,
    starts_ref,
    states_ref,
):
    lane = lax.broadcasted_iota(jnp.int32, (PIECES, LANES), 1)
    piece = lax.broadcasted_iota(jnp.int32, (PIECES, LANES), 0)
    zero = jnp.zeros((PIECES, LANES), jnp.float32)

    def forward(step, state):
        x = vector_at(x_ref, step)
        if left_ref.shape[0] == PIECES:
            before, after = [], []
            for c in SIZES:
                place = jnp.full((PIECES, LANES), step * COMP + c, jnp.int32)
                for out, edges_ref, turn, at in (
                    (before, left_ref, 1, 0),
                    (after, right_ref, LANES - 1, LANES - 1),
                ):
                    edge = jnp.take_along_axis(
                        edges_ref[...], place, axis=1, mode="promise_in_bounds"
                    )
                    out.append(jnp.where(lane == at, edge, pltpu.roll(x[c], turn, 1)))
        else:
            before = [
                pltpu.roll(jnp.where(lane == LANES - 1, a, b), 1, 1)
                for a, b in zip(vector_at(left_ref, step), x)
            ]
            after = [
                pltpu.roll(jnp.where(lane == 0, a, b), LANES - 1, 1)
                for a, b in zip(vector_at(right_ref, step), x)
            ]
        near = [vector_at(below_ref, step), vector_at(above_ref, step), before, after]
        rhs = vector_at(source_ref, step)
        for direc in range(4):
            block = block_at(coupling_ref, step, direc * POINTS * BLOCK)
            for c in SIZES:
                rhs[c] = rhs[c] - total([block[e][c] * near[direc][e] for e in SIZES])
        flag = iblank_ref[pl.ds(step, PIECES, stride=STEPS), :]
        donated = packed_at(donated_ref, step)
        rhs = [
            jnp.where(flag == 0, 0.0, a + jnp.where(flag == 2, b, 0.0))
            for a, b in zip(rhs, donated)
        ]
        scaled = times(block_at(pivot_ref, step), rhs)
        put_packed(scaled_ref, step, scaled)
        state = less(scaled, times(block_at(lower_ref, step), state))
        put_packed(states_ref, step, state)
        return tuple(state)

    ahead = list(lax.fori_loop(0, STEPS, forward, (zero,) * COMP))

    def backward(count, state):
        step = STEPS - 1 - count
        y = packed_at(states_ref, step)
        return tuple(less(y, times(block_at(upper_ref, step), state)))

    behind = list(lax.fori_loop(0, STEPS, backward, (zero,) * COMP))

    for level, shift in enumerate((1, 2, 4)):
        ahead = add(ahead, times(map_at(maps_ref, FWD0 + level), [moved(a, shift) for a in ahead]))
    entry = [jnp.where(piece == 0, 0.0, moved(a, 1)) for a in ahead]
    behind = add(behind, times(map_at(maps_ref, FOLD), entry))
    for level, shift in enumerate((1, 2, 4)):
        behind = add(
            behind, times(map_at(maps_ref, BWD0 + level), [moved(a, -shift) for a in behind])
        )
    put_packed(starts_ref, 0, entry)
    put_packed(
        starts_ref, 1, [jnp.where(piece == PIECES - 1, 0.0, moved(a, -1)) for a in behind]
    )
    y_out = [jnp.broadcast_to(a[PIECES - 1 :, :], (COMP, LANES)) for a in ahead]
    x_out = [jnp.broadcast_to(a[:1, :], (COMP, LANES)) for a in behind]
    row = lax.broadcasted_iota(jnp.int32, (COMP, LANES), 0)

    def stacked(rows):
        out = rows[0]
        for c in SIZES[1:]:
            out = jnp.where(row == c, rows[c], out)
        return out

    def outer(which, rows):
        return total([outer_ref[pl.ds((which * COMP + e) * PIECES, COMP), :] * rows[e] for e in SIZES])

    inside = stacked(y_out), stacked(x_out)
    outside = outer(0, y_out), outer(1, y_out) + outer(2, x_out)
    mine = lax.axis_index("normal") // MEMBERS
    slot = VALUES if share_ref is None else SLOT
    for device in range(count):
        same = mine == device // MEMBERS
        for k in range(2):
            at = device * slot + k * COMP
            sent_ref[pl.ds(at, COMP), :] = jnp.where(same, inside[k], outside[k])
        if share_ref is not None:
            sent_ref[pl.ds(device * slot + VALUES, SHARE), :] = share_ref[pl.ds(0, SHARE), :]


def solve_without(count, *refs):
    solve_kernel(count, *refs[:14], None, *refs[14:])


def group_maps(members_ref, share_ref, outer_ref, whole_ref, work_ref):
    own = lax.rem(lax.axis_index("normal"), MEMBERS)
    row = lax.broadcasted_iota(jnp.int32, (COMP, LANES), 0)
    eye = [jnp.where(row == e, 1.0, 0.0) for e in SIZES]
    none = [jnp.zeros((COMP, LANES), jnp.float32)] * COMP

    def given(member, which):
        base = member * PADDED + which * BLOCK
        columns = [members_ref[pl.ds(base + e, COMP, stride=COMP), :] for e in SIZES]
        return columns, lambda k, e: members_ref[pl.ds(base + k * COMP + e, 1), :]

    def kept(columns, place):
        for e in SIZES:
            work_ref[pl.ds((place * COMP + e) * PIECES, COMP), :] = columns[e]
        return lambda k, e: work_ref[pl.ds((place * COMP + e) * PIECES + k, 1), :]

    def multiply(columns, element):
        return [total([columns[k] * element(k, e) for k in SIZES]) for e in SIZES]

    def chosen(options):
        out = options[-1]
        for member in range(MEMBERS - 1):
            out = [jnp.where(own == member, a, b) for a, b in zip(options[member], out)]
        return out

    onward, across = [given(MEMBERS - 1, 0)[0]], [given(MEMBERS - 1, 1)[0]]
    for member in range(MEMBERS - 2, -1, -1):
        forward = given(member, 0)[1]
        onward.insert(0, multiply(onward[0], forward))
        inner = kept(multiply(across[0], forward), member)
        across.insert(0, add(given(member, 1)[0], multiply(given(member, 2)[0], inner)))
    back = [eye, given(0, 2)[0]]
    for member in range(1, MEMBERS):
        back.append(multiply(back[-1], given(member, 2)[1]))
    mixed = multiply(
        chosen(back[1:MEMBERS] + [none]), kept(chosen(across[1:] + [none]), MEMBERS - 1)
    )
    for k, columns in enumerate((chosen(onward[1:] + [eye]), mixed, chosen(back[:MEMBERS]))):
        for e in SIZES:
            outer_ref[pl.ds((k * COMP + e) * PIECES, COMP), :] = columns[e]
    for k, columns in enumerate((onward[0], across[0], back[MEMBERS])):
        for e in SIZES:
            whole_ref[pl.ds(k * BLOCK + e, COMP, stride=COMP), :] = columns[e]
    whole_ref[pl.ds(ROWS, 1), :] = jnp.zeros((1, LANES), jnp.float32)
    share_ref[pl.ds(0, SHARE), :] = whole_ref[pl.ds(own * SHARE, SHARE), :]


def finish_kernel(
    count,
    slot,
    values_ref,
    shares_ref,
    members_ref,
    lower_ref,
    upper_ref,
    maps_ref,
    scaled_ref,
    starts_ref,
    out_ref,
    first_ref,
    last_ref,
    states_ref,
    entry_ref,
):
    me = lax.axis_index("normal")
    mine, own = me // MEMBERS, lax.rem(me, MEMBERS)
    groups = count // MEMBERS

    def group_map(group, which):
        def row(at):
            place = (group * MEMBERS + at // SHARE) * SLOT + VALUES + at % SHARE
            return shares_ref[pl.ds(place, 1), :]

        return [[row((which * COMP + c) * COMP + e) for e in SIZES] for c in SIZES]

    def member_map(member, which):
        base = member * PADDED + which * BLOCK
        return [[members_ref[pl.ds(base + c * COMP + e, 1), :] for e in SIZES] for c in SIZES]

    def value(device, which):
        return [values_ref[pl.ds(device * slot + which * COMP + c, 1), :] for c in SIZES]

    def group_value(group, which):
        parts = [value(group * MEMBERS + member, which) for member in range(MEMBERS)]
        return [total([part[c] for part in parts]) for c in SIZES]

    def put_entry(at, state):
        for c in SIZES:
            entry_ref[pl.ds(at * PIECES + c, 1), :] = state[c]

    def entry(at):
        return [entry_ref[pl.ds(at * PIECES + c, 1), :] for c in SIZES]

    none = (jnp.zeros((1, LANES), jnp.float32),) * COMP

    def over_group(group, state):
        put_entry(group, state)
        return tuple(add(group_value(group, 0), times(group_map(group, 0), list(state))))

    state = lax.fori_loop(0, mine, over_group, none)
    for member in range(MEMBERS):
        put_entry(groups + member, state)
        state = add(value(mine * MEMBERS + member, 0), times(member_map(member, 0), list(state)))
    lax.fori_loop(mine + 1, groups, over_group, tuple(state))

    def back_over_group(step, state):
        group = groups - 1 - step
        inner = add(group_value(group, 1), times(group_map(group, 1), entry(group)))
        return tuple(add(inner, times(group_map(group, 2), list(state))))

    state = lax.fori_loop(0, groups - 1 - mine, back_over_group, none)

    def back_over_member(step, state):
        member = MEMBERS - 1 - step
        inner = add(
            value(mine * MEMBERS + member, 1), times(member_map(member, 1), entry(groups + member))
        )
        return tuple(add(inner, times(member_map(member, 2), list(state))))

    x_in = lax.fori_loop(0, MEMBERS - 1 - own, back_over_member, state)

    y_in = [jnp.broadcast_to(a, (PIECES, LANES)) for a in entry(groups + own)]
    x_in = [jnp.broadcast_to(a, (PIECES, LANES)) for a in x_in]

    y_start = add(packed_at(starts_ref, 0), times(map_at(maps_ref, HEAD), y_in))
    x_start = add(packed_at(starts_ref, 1), times(map_at(maps_ref, FROM_Y), y_in))
    x_start = add(x_start, times(map_at(maps_ref, FROM_X), x_in))

    def ahead(step, state):
        state = less(packed_at(scaled_ref, step), times(block_at(lower_ref, step), list(state)))
        put_packed(states_ref, step, state)
        return tuple(state)

    lax.fori_loop(0, STEPS, ahead, tuple(y_start))

    def behind(turn, carry):
        state, edges = carry
        step = STEPS - 1 - turn
        state = less(packed_at(states_ref, step), times(block_at(upper_ref, step), list(state)))
        for c in SIZES:
            out_ref[pl.ds(step * COMP + c, PIECES, stride=STEPS * COMP), :] = state[c]
        if first_ref is not None:
            edges = with_edges(state, step, *edges)
        return tuple(state), edges

    edges = () if first_ref is None else no_edges()
    _, edges = lax.fori_loop(0, STEPS, behind, (tuple(x_start), edges))
    if first_ref is not None:
        first_ref[...], last_ref[...] = edges


def finish_without(count, slot, *refs):
    finish_kernel(count, slot, *refs[:9], None, None, *refs[9:])


def floats(rows):
    return jax.ShapeDtypeStruct((rows, LANES), jnp.float32)


def scratch(rows):
    return pltpu.VMEM((rows, LANES), jnp.float32)


def call(kernel, inputs, outputs, scratches, name, micros, far=()):
    hbm = pl.BlockSpec(memory_space=pltpu.HBM)
    places = range(len(inputs) + len(outputs))
    specs = [hbm if k in far else VMEM for k in places]
    inputs = [
        pltpu.with_memory_space_constraint(a, pltpu.HBM) if k in far else a
        for k, a in enumerate(inputs)
    ]
    return pl.pallas_call(
        kernel,
        out_shape=[floats(a) if isinstance(a, int) else a for a in outputs],
        in_specs=specs[: len(inputs)],
        out_specs=specs[len(inputs) :],
        scratch_shapes=[scratch(a) if isinstance(a, int) else a for a in scratches],
        compiler_params=pltpu.CompilerParams(vmem_limit_bytes=16 << 20),
        cost_estimate=pl.CostEstimate(
            flops=0, bytes_accessed=int(micros * 3.0e6), transcendentals=0
        ),
        name=name,
    )(*inputs)


def ring(count, step):
    return [(i, (i + step) % count) for i in range(count)]


def per_device(iterate, source, pivot, lower, upper, coupling, iblank, donor):
    count = lax.axis_size("normal")
    x = iterate.reshape(-1, LANES)
    source, pivot, lower, upper, coupling, iblank, donor = (
        a.reshape(-1, LANES) for a in (source, pivot, lower, upper, coupling, iblank, donor)
    )
    field = POINTS * COMP
    state = STEPS * COMP * PIECES

    def both(up, down, axis):
        size = lax.axis_size(axis)
        return [lax.ppermute(up, axis, ring(size, 1)), lax.ppermute(down, axis, ring(size, -1))]

    def exchanged(rows, parts, groups=None):
        rows = rows.reshape(parts, -1, 1, LANES)
        return lax.all_to_all(rows, "normal", 0, 0, axis_index_groups=groups).reshape(-1, LANES)

    maps_rows = MAPS * BLOCK * PIECES
    local_rows = STEPS * BLOCK * PIECES
    whole_rows = MEMBERS * PADDED
    entries = (count // MEMBERS + MEMBERS) * PIECES

    (whole,) = call(
        summary_kernel,
        (lower, upper),
        (whole_rows,),
        (
            lower.shape[0],
            upper.shape[0],
            maps_rows,
            whole_rows,
            local_rows,
            pltpu.SemaphoreType.DMA((3,)),
        ),
        "summary",
        2,
        far=(0, 1, 2),
    )
    groups = [list(range(k, k + MEMBERS)) for k in range(0, count, MEMBERS)]
    members = exchanged(whole, MEMBERS, groups)
    near = both(x, x, "span") + both(x, x, "stream")
    given = (lower, upper, x, donor, source, pivot, coupling, iblank)
    *given, donated, maps, share, outer = call(
        start_kernel,
        (members, *given),
        [jax.ShapeDtypeStruct(a.shape, a.dtype) for a in given]
        + [state, maps_rows, 24, 3 * COMP * PIECES],
        (
            whole_rows,
            local_rows,
            PADDED + 4,
            MEMBERS * COMP * PIECES,
            pltpu.SemaphoreType.DMA((len(given),)),
        ),
        "start",
        4,
        far=range(1, len(given) + 1),
    )
    lower, upper, x, donor, source, pivot, coupling, iblank = given
    fixed = (source, pivot, lower, upper, coupling, iblank)
    sent, scaled, starts = call(
        functools.partial(solve_kernel, count),
        (x, *near, *fixed, donated, maps, outer, share),
        (count * SLOT, state, 2 * COMP * PIECES),
        (state,),
        "solve",
        2,
    )
    shares = exchanged(sent, count)
    x, first, last = call(
        functools.partial(finish_kernel, count, SLOT),
        (shares, shares, members, lower, upper, maps, scaled, starts),
        (field, PIECES, PIECES),
        (state, entries),
        "finish",
        1,
    )

    near = both(x, x, "span") + both(last, first, "stream")
    (donated,) = call(donate_kernel, (x, donor), (state,), (), "donate", 2)
    sent, scaled, starts = call(
        functools.partial(solve_without, count),
        (x, *near, *fixed, donated, maps, outer),
        (count * VALUES, state, 2 * COMP * PIECES),
        (state,),
        "solve",
        2,
    )
    values = exchanged(sent, count)
    (x,) = call(
        functools.partial(finish_without, count, VALUES),
        (values, shares, members, lower, upper, maps, scaled, starts),
        (field,),
        (state, entries),
        "finish",
        1,
    )
    return x.reshape(iterate.shape)


def solution(mesh):
    placed = (
        P("normal", None, "span", "stream"),
        P("normal", None, "span", "stream"),
        P("normal", None, None, "span", "stream"),
        P("normal", None, None, "span", "stream"),
        P("normal", None, None, "span", "stream"),
        P(None, "normal", None, None, "span", "stream"),
        P("normal", "span", "stream"),
        P("normal", "span", "stream"),
    )
    return jax.shard_map(
        per_device,
        mesh=mesh,
        in_specs=placed,
        out_specs=P("normal", None, "span", "stream"),
        check_vma=False,
    )
```

```python
import functools

import jax
import jax.numpy as jnp
from jax import lax
from jax.experimental import pallas as pl
from jax.experimental.pallas import tpu as pltpu
from jax.sharding import PartitionSpec as P

COMP = 5
BLOCK = COMP * COMP
PIECES = 8
LANES = 128
STEPS = 6
POINTS = PIECES * STEPS
SIZES = range(COMP)
FWD0, FWD1, FWD2, BWD0, BWD1, BWD2, FOLD, HEAD, FROM_Y, FROM_X = range(10)
MAPS = 10
ROWS = 3 * BLOCK
VALUES = 2 * COMP
MEMBERS = 4
PADDED = 76
SHARE = PADDED // MEMBERS
SLOT = VALUES + SHARE
VMEM = pl.BlockSpec(memory_space=pltpu.VMEM)


def vector_at(ref, step):
    return [ref[pl.ds(step * COMP + c, PIECES, stride=STEPS * COMP), :] for c in SIZES]


def block_at(ref, step, base=0):
    start = base + step * BLOCK
    return [
        [ref[pl.ds(start + c * COMP + e, PIECES, stride=STEPS * BLOCK), :] for e in SIZES]
        for c in SIZES
    ]


def packed_at(ref, step):
    return [ref[pl.ds((step * COMP + c) * PIECES, PIECES), :] for c in SIZES]


def put_packed(ref, step, value):
    for c in SIZES:
        ref[pl.ds((step * COMP + c) * PIECES, PIECES), :] = value[c]


def map_at(ref, which):
    return [
        [ref[pl.ds(((which * COMP + c) * COMP + e) * PIECES, PIECES), :] for e in SIZES]
        for c in SIZES
    ]


def put_map(ref, which, value):
    for c in SIZES:
        for e in SIZES:
            ref[pl.ds(((which * COMP + c) * COMP + e) * PIECES, PIECES), :] = value[c][e]


def total(terms):
    while len(terms) > 1:
        terms = [sum(terms[k : k + 2][1:], terms[k]) for k in range(0, len(terms), 2)]
    return terms[0]


def times(block, vector):
    return [total([block[c][e] * vector[e] for e in SIZES]) for c in SIZES]


def product(left, right):
    return [
        [total([left[c][k] * right[k][e] for k in SIZES]) for e in SIZES] for c in SIZES
    ]


def each(function, *maps):
    return [[function(*(m[c][e] for m in maps)) for e in SIZES] for c in SIZES]


def add(left, right):
    return [a + b for a, b in zip(left, right)]


def less(left, right):
    return [a - b for a, b in zip(left, right)]


def moved(value, steps):
    return pltpu.roll(value, steps % PIECES, 0)


def donate(x_ref, donor_ref, donated_ref):
    lanes, rows = [], []
    for step in range(STEPS):
        place = donor_ref[pl.ds(step, PIECES, stride=STEPS), :]
        lanes.append(place & (LANES - 1))
        rows.append(place >> 7)

    zero = jnp.zeros((PIECES, LANES), jnp.float32)
    for step in range(STEPS):
        found = [zero] * COMP
        for row in range(POINTS):
            here = rows[step] == row
            for c in SIZES:
                line = jnp.broadcast_to(x_ref[pl.ds(row * COMP + c, 1), :], (PIECES, LANES))
                picked = jnp.take_along_axis(line, lanes[step], axis=1, mode="promise_in_bounds")
                found[c] = jnp.where(here, picked, found[c])
        put_packed(donated_ref, step, found)


def donate_kernel(x_ref, donor_ref, donated_ref):
    donate(x_ref, donor_ref, donated_ref)


def edges_of(ref):
    lane = lax.broadcasted_iota(jnp.int32, (PIECES, LANES), 1)
    first = last = jnp.zeros((PIECES, LANES), jnp.float32)
    for step in range(STEPS):
        for c, value in enumerate(vector_at(ref, step)):
            here = lane == step * COMP + c
            first = jnp.where(here, jnp.broadcast_to(value[:, :1], (PIECES, LANES)), first)
            last = jnp.where(here, jnp.broadcast_to(value[:, -1:], (PIECES, LANES)), last)
    return first, last


def summary_kernel(*refs):
    given, results, kept, (maps_ref, local_ref, moves) = refs[:3], refs[3:6], refs[6:12], refs[12:]
    coming = [pltpu.make_async_copy(a, b, moves.at[k]) for k, (a, b) in enumerate(zip(given, kept))]
    leaving = [
        pltpu.make_async_copy(a, b, moves.at[3 + k]) for k, (a, b) in enumerate(zip(kept[3:], results))
    ]
    x_ref, lower_ref, upper_ref, first_ref, last_ref, whole_ref = kept
    for copy in coming:
        copy.start()
    coming[0].wait()
    first_ref[...], last_ref[...] = edges_of(x_ref)
    for copy in leaving[:2]:
        copy.start()
    for copy in coming[1:]:
        copy.wait()
    make_maps(lower_ref, upper_ref, maps_ref, whole_ref, local_ref)
    leaving[2].start()
    for copy in leaving:
        copy.wait()


def start_kernel(*refs):
    members_ref, given, kept = refs[0], refs[1:9], refs[9:17]
    donated_ref, maps_ref, share_ref, outer_ref = refs[17:21]
    whole_ref, local_ref, group_ref, work_ref, arrived = refs[21:]
    copies = [
        pltpu.make_async_copy(a, b, arrived.at[k]) for k, (a, b) in enumerate(zip(given, kept))
    ]
    for copy in copies:
        copy.start()
    x_ref, donor_ref, lower_ref, upper_ref = kept[:4]
    group_maps(members_ref, share_ref, outer_ref, group_ref, work_ref)
    for copy in copies[:2]:
        copy.wait()
    donate(x_ref, donor_ref, donated_ref)
    for copy in copies[2:4]:
        copy.wait()
    make_maps(lower_ref, upper_ref, maps_ref, whole_ref, local_ref)
    for copy in copies[4:]:
        copy.wait()


def put_whole(ref, at, row):
    for member in range(MEMBERS):
        ref[pl.ds(member * PADDED + at, 1), :] = row


def make_maps(lower_ref, upper_ref, maps_ref, whole_ref, local_ref):
    piece = lax.broadcasted_iota(jnp.int32, (PIECES, LANES), 0)
    one = jnp.ones((PIECES, LANES), jnp.float32)
    zero = jnp.zeros((PIECES, LANES), jnp.float32)
    eye = [[one if c == e else zero for e in SIZES] for c in SIZES]

    def pack(value):
        return tuple(value[c][e] for c in SIZES for e in SIZES)

    def unpack(flat):
        return [list(flat[c * COMP : (c + 1) * COMP]) for c in SIZES]

    first = each(lambda a: -a, block_at(lower_ref, 0))
    put_map(local_ref, 0, first)

    def forward(step, state):
        block = block_at(lower_ref, step)
        state = each(lambda a: -a, product(block, unpack(state)))
        put_map(local_ref, step, state)
        return pack(state)

    ahead = unpack(lax.fori_loop(1, STEPS, forward, pack(first)))

    def backward(count, carry):
        behind, fold = unpack(carry[:BLOCK]), unpack(carry[BLOCK:])
        step = STEPS - 1 - count
        block = block_at(upper_ref, step)
        behind = each(lambda a: -a, product(block, behind))
        fold = each(lambda a, b: a - b, map_at(local_ref, step), product(block, fold))
        return pack(behind) + pack(fold)

    last = block_at(upper_ref, STEPS - 1)
    start = pack(each(lambda a: -a, last)) + pack(map_at(local_ref, STEPS - 1))
    carry = lax.fori_loop(1, STEPS, backward, start)
    behind, fold = unpack(carry[:BLOCK]), unpack(carry[BLOCK:])
    put_map(maps_ref, FOLD, fold)

    window = ahead
    for level, shift in enumerate((1, 2, 4)):
        inside = piece >= shift
        put_map(maps_ref, FWD0 + level, each(lambda a: jnp.where(inside, a, 0.0), window))
        longer = product(window, each(lambda a: moved(a, shift), window))
        window = each(lambda a, b: jnp.where(inside, a, b), longer, window)
    head = each(lambda a, b: jnp.where(piece == 0, b, moved(a, 1)), window, eye)
    put_map(maps_ref, HEAD, head)
    for c in SIZES:
        for e in SIZES:
            put_whole(whole_ref, c * COMP + e, window[c][e][PIECES - 1 :, :])

    window = behind
    response = product(fold, head)
    for level, shift in enumerate((1, 2, 4)):
        inside = piece < PIECES - shift
        masked = each(lambda a: jnp.where(inside, a, 0.0), window)
        put_map(maps_ref, BWD0 + level, masked)
        response = each(
            lambda a, b: a + b,
            response,
            product(masked, each(lambda a: moved(a, -shift), response)),
        )
        longer = product(window, each(lambda a: moved(a, -shift), window))
        window = each(lambda a, b: jnp.where(inside, a, b), longer, window)
    final = piece == PIECES - 1
    put_map(maps_ref, FROM_Y, each(lambda a: jnp.where(final, 0.0, moved(a, -1)), response))
    put_map(maps_ref, FROM_X, each(lambda a, b: jnp.where(final, b, moved(a, -1)), window, eye))
    for c in SIZES:
        for e in SIZES:
            at = c * COMP + e
            put_whole(whole_ref, BLOCK + at, response[c][e][:1, :])
            put_whole(whole_ref, 2 * BLOCK + at, window[c][e][:1, :])
    put_whole(whole_ref, ROWS, jnp.zeros((1, LANES), jnp.float32))


def solve_kernel(
    count,
    x_ref,
    below_ref,
    above_ref,
    left_ref,
    right_ref,
    source_ref,
    pivot_ref,
    lower_ref,
    upper_ref,
    coupling_ref,
    iblank_ref,
    donated_ref,
    maps_ref,
    outer_ref,
    share_ref,
    sent_ref,
    scaled_ref,
    starts_ref,
    states_ref,
):
    lane = lax.broadcasted_iota(jnp.int32, (PIECES, LANES), 1)
    piece = lax.broadcasted_iota(jnp.int32, (PIECES, LANES), 0)
    zero = jnp.zeros((PIECES, LANES), jnp.float32)

    def forward(step, state):
        x = vector_at(x_ref, step)
        before, after = [], []
        for c in SIZES:
            place = jnp.full((PIECES, LANES), step * COMP + c, jnp.int32)
            for out, edges_ref, turn, at in (
                (before, left_ref, 1, 0),
                (after, right_ref, LANES - 1, LANES - 1),
            ):
                edge = jnp.take_along_axis(edges_ref[...], place, axis=1, mode="promise_in_bounds")
                out.append(jnp.where(lane == at, edge, pltpu.roll(x[c], turn, 1)))
        near = [vector_at(below_ref, step), vector_at(above_ref, step), before, after]
        rhs = vector_at(source_ref, step)
        for direc in range(4):
            block = block_at(coupling_ref, step, direc * POINTS * BLOCK)
            for c in SIZES:
                rhs[c] = rhs[c] - total([block[e][c] * near[direc][e] for e in SIZES])
        flag = iblank_ref[pl.ds(step, PIECES, stride=STEPS), :]
        donated = packed_at(donated_ref, step)
        rhs = [
            jnp.where(flag == 0, 0.0, a + jnp.where(flag == 2, b, 0.0))
            for a, b in zip(rhs, donated)
        ]
        scaled = times(block_at(pivot_ref, step), rhs)
        put_packed(scaled_ref, step, scaled)
        state = less(scaled, times(block_at(lower_ref, step), state))
        put_packed(states_ref, step, state)
        return tuple(state)

    ahead = list(lax.fori_loop(0, STEPS, forward, (zero,) * COMP))

    def backward(count, state):
        step = STEPS - 1 - count
        y = packed_at(states_ref, step)
        return tuple(less(y, times(block_at(upper_ref, step), state)))

    behind = list(lax.fori_loop(0, STEPS, backward, (zero,) * COMP))

    for level, shift in enumerate((1, 2, 4)):
        ahead = add(ahead, times(map_at(maps_ref, FWD0 + level), [moved(a, shift) for a in ahead]))
    entry = [jnp.where(piece == 0, 0.0, moved(a, 1)) for a in ahead]
    behind = add(behind, times(map_at(maps_ref, FOLD), entry))
    for level, shift in enumerate((1, 2, 4)):
        behind = add(
            behind, times(map_at(maps_ref, BWD0 + level), [moved(a, -shift) for a in behind])
        )
    put_packed(starts_ref, 0, entry)
    put_packed(
        starts_ref, 1, [jnp.where(piece == PIECES - 1, 0.0, moved(a, -1)) for a in behind]
    )
    y_out = [jnp.broadcast_to(a[PIECES - 1 :, :], (COMP, LANES)) for a in ahead]
    x_out = [jnp.broadcast_to(a[:1, :], (COMP, LANES)) for a in behind]
    row = lax.broadcasted_iota(jnp.int32, (COMP, LANES), 0)

    def stacked(rows):
        out = rows[0]
        for c in SIZES[1:]:
            out = jnp.where(row == c, rows[c], out)
        return out

    def outer(which, rows):
        return total([outer_ref[pl.ds((which * COMP + e) * PIECES, COMP), :] * rows[e] for e in SIZES])

    inside = stacked(y_out), stacked(x_out)
    outside = outer(0, y_out), outer(1, y_out) + outer(2, x_out)
    mine = lax.axis_index("normal") // MEMBERS
    slot = VALUES if share_ref is None else SLOT
    for device in range(count):
        same = mine == device // MEMBERS
        for k in range(2):
            at = device * slot + k * COMP
            sent_ref[pl.ds(at, COMP), :] = jnp.where(same, inside[k], outside[k])
        if share_ref is not None:
            sent_ref[pl.ds(device * slot + VALUES, SHARE), :] = share_ref[pl.ds(0, SHARE), :]


def solve_without(count, *refs):
    solve_kernel(count, *refs[:14], None, *refs[14:])


def group_maps(members_ref, share_ref, outer_ref, whole_ref, work_ref):
    own = lax.rem(lax.axis_index("normal"), MEMBERS)
    row = lax.broadcasted_iota(jnp.int32, (COMP, LANES), 0)
    eye = [jnp.where(row == e, 1.0, 0.0) for e in SIZES]
    none = [jnp.zeros((COMP, LANES), jnp.float32)] * COMP

    def given(member, which):
        base = member * PADDED + which * BLOCK
        columns = [members_ref[pl.ds(base + e, COMP, stride=COMP), :] for e in SIZES]
        return columns, lambda k, e: members_ref[pl.ds(base + k * COMP + e, 1), :]

    def kept(columns, place):
        for e in SIZES:
            work_ref[pl.ds((place * COMP + e) * PIECES, COMP), :] = columns[e]
        return lambda k, e: work_ref[pl.ds((place * COMP + e) * PIECES + k, 1), :]

    def multiply(columns, element):
        return [total([columns[k] * element(k, e) for k in SIZES]) for e in SIZES]

    def chosen(options):
        out = options[-1]
        for member in range(MEMBERS - 1):
            out = [jnp.where(own == member, a, b) for a, b in zip(options[member], out)]
        return out

    onward, across = [given(MEMBERS - 1, 0)[0]], [given(MEMBERS - 1, 1)[0]]
    for member in range(MEMBERS - 2, -1, -1):
        forward = given(member, 0)[1]
        onward.insert(0, multiply(onward[0], forward))
        inner = kept(multiply(across[0], forward), member)
        across.insert(0, add(given(member, 1)[0], multiply(given(member, 2)[0], inner)))
    back = [eye, given(0, 2)[0]]
    for member in range(1, MEMBERS):
        back.append(multiply(back[-1], given(member, 2)[1]))
    mixed = multiply(
        chosen(back[1:MEMBERS] + [none]), kept(chosen(across[1:] + [none]), MEMBERS - 1)
    )
    for k, columns in enumerate((chosen(onward[1:] + [eye]), mixed, chosen(back[:MEMBERS]))):
        for e in SIZES:
            outer_ref[pl.ds((k * COMP + e) * PIECES, COMP), :] = columns[e]
    for k, columns in enumerate((onward[0], across[0], back[MEMBERS])):
        for e in SIZES:
            whole_ref[pl.ds(k * BLOCK + e, COMP, stride=COMP), :] = columns[e]
    whole_ref[pl.ds(ROWS, 1), :] = jnp.zeros((1, LANES), jnp.float32)
    share_ref[pl.ds(0, SHARE), :] = whole_ref[pl.ds(own * SHARE, SHARE), :]


def finish_kernel(
    count,
    slot,
    values_ref,
    shares_ref,
    members_ref,
    lower_ref,
    upper_ref,
    maps_ref,
    scaled_ref,
    starts_ref,
    out_ref,
    first_ref,
    last_ref,
    states_ref,
    entry_ref,
):
    me = lax.axis_index("normal")
    mine, own = me // MEMBERS, lax.rem(me, MEMBERS)
    groups = count // MEMBERS

    def group_map(group, which):
        def row(at):
            place = (group * MEMBERS + at // SHARE) * SLOT + VALUES + at % SHARE
            return shares_ref[pl.ds(place, 1), :]

        return [[row((which * COMP + c) * COMP + e) for e in SIZES] for c in SIZES]

    def member_map(member, which):
        base = member * PADDED + which * BLOCK
        return [[members_ref[pl.ds(base + c * COMP + e, 1), :] for e in SIZES] for c in SIZES]

    def value(device, which):
        return [values_ref[pl.ds(device * slot + which * COMP + c, 1), :] for c in SIZES]

    def group_value(group, which):
        parts = [value(group * MEMBERS + member, which) for member in range(MEMBERS)]
        return [total([part[c] for part in parts]) for c in SIZES]

    def put_entry(at, state):
        for c in SIZES:
            entry_ref[pl.ds(at * PIECES + c, 1), :] = state[c]

    def entry(at):
        return [entry_ref[pl.ds(at * PIECES + c, 1), :] for c in SIZES]

    none = (jnp.zeros((1, LANES), jnp.float32),) * COMP

    def over_group(group, state):
        put_entry(group, state)
        return tuple(add(group_value(group, 0), times(group_map(group, 0), list(state))))

    state = lax.fori_loop(0, mine, over_group, none)
    for member in range(MEMBERS):
        put_entry(groups + member, state)
        state = add(value(mine * MEMBERS + member, 0), times(member_map(member, 0), list(state)))
    lax.fori_loop(mine + 1, groups, over_group, tuple(state))

    def back_over_group(step, state):
        group = groups - 1 - step
        inner = add(group_value(group, 1), times(group_map(group, 1), entry(group)))
        return tuple(add(inner, times(group_map(group, 2), list(state))))

    state = lax.fori_loop(0, groups - 1 - mine, back_over_group, none)

    def back_over_member(step, state):
        member = MEMBERS - 1 - step
        inner = add(
            value(mine * MEMBERS + member, 1), times(member_map(member, 1), entry(groups + member))
        )
        return tuple(add(inner, times(member_map(member, 2), list(state))))

    x_in = lax.fori_loop(0, MEMBERS - 1 - own, back_over_member, state)

    y_in = [jnp.broadcast_to(a, (PIECES, LANES)) for a in entry(groups + own)]
    x_in = [jnp.broadcast_to(a, (PIECES, LANES)) for a in x_in]

    y_start = add(packed_at(starts_ref, 0), times(map_at(maps_ref, HEAD), y_in))
    x_start = add(packed_at(starts_ref, 1), times(map_at(maps_ref, FROM_Y), y_in))
    x_start = add(x_start, times(map_at(maps_ref, FROM_X), x_in))

    def ahead(step, state):
        state = less(packed_at(scaled_ref, step), times(block_at(lower_ref, step), list(state)))
        put_packed(states_ref, step, state)
        return tuple(state)

    lax.fori_loop(0, STEPS, ahead, tuple(y_start))

    def behind(turn, state):
        step = STEPS - 1 - turn
        state = less(packed_at(states_ref, step), times(block_at(upper_ref, step), list(state)))
        for c in SIZES:
            out_ref[pl.ds(step * COMP + c, PIECES, stride=STEPS * COMP), :] = state[c]
        return tuple(state)

    lax.fori_loop(0, STEPS, behind, tuple(x_start))
    if first_ref is not None:
        first_ref[...], last_ref[...] = edges_of(out_ref)


def finish_without(count, slot, *refs):
    finish_kernel(count, slot, *refs[:9], None, None, *refs[9:])


def floats(rows):
    return jax.ShapeDtypeStruct((rows, LANES), jnp.float32)


def scratch(rows):
    return pltpu.VMEM((rows, LANES), jnp.float32)


def call(kernel, inputs, outputs, scratches, name, micros, far=()):
    hbm = pl.BlockSpec(memory_space=pltpu.HBM)
    places = range(len(inputs) + len(outputs))
    specs = [hbm if k in far else VMEM for k in places]
    inputs = [
        pltpu.with_memory_space_constraint(a, pltpu.HBM) if k in far else a
        for k, a in enumerate(inputs)
    ]
    return pl.pallas_call(
        kernel,
        out_shape=[floats(a) if isinstance(a, int) else a for a in outputs],
        in_specs=specs[: len(inputs)],
        out_specs=specs[len(inputs) :],
        scratch_shapes=[scratch(a) if isinstance(a, int) else a for a in scratches],
        compiler_params=pltpu.CompilerParams(vmem_limit_bytes=16 << 20),
        cost_estimate=pl.CostEstimate(
            flops=0, bytes_accessed=int(micros * 3.0e6), transcendentals=0
        ),
        name=name,
    )(*inputs)


def ring(count, step):
    return [(i, (i + step) % count) for i in range(count)]


def per_device(iterate, source, pivot, lower, upper, coupling, iblank, donor):
    count = lax.axis_size("normal")
    x = iterate.reshape(-1, LANES)
    source, pivot, lower, upper, coupling, iblank, donor = (
        a.reshape(-1, LANES) for a in (source, pivot, lower, upper, coupling, iblank, donor)
    )
    field = POINTS * COMP
    state = STEPS * COMP * PIECES

    def both(up, down, axis):
        size = lax.axis_size(axis)
        return [lax.ppermute(up, axis, ring(size, 1)), lax.ppermute(down, axis, ring(size, -1))]

    def exchanged(rows, parts, groups=None):
        rows = rows.reshape(parts, -1, 1, LANES)
        return lax.all_to_all(rows, "normal", 0, 0, axis_index_groups=groups).reshape(-1, LANES)

    maps_rows = MAPS * BLOCK * PIECES
    local_rows = STEPS * BLOCK * PIECES
    whole_rows = MEMBERS * PADDED
    entries = (count // MEMBERS + MEMBERS) * PIECES

    first, last, whole = call(
        summary_kernel,
        (x, lower, upper),
        (PIECES, PIECES, whole_rows),
        (
            x.shape[0],
            lower.shape[0],
            upper.shape[0],
            PIECES,
            PIECES,
            whole_rows,
            maps_rows,
            local_rows,
            pltpu.SemaphoreType.DMA((6,)),
        ),
        "summary",
        2,
        far=range(6),
    )
    groups = [list(range(k, k + MEMBERS)) for k in range(0, count, MEMBERS)]
    members = exchanged(whole, MEMBERS, groups)
    near = both(x, x, "span") + both(last, first, "stream")
    given = (x, donor, lower, upper, source, pivot, coupling, iblank)
    *given, donated, maps, share, outer = call(
        start_kernel,
        (members, *given),
        [jax.ShapeDtypeStruct(a.shape, a.dtype) for a in given]
        + [state, maps_rows, 24, 3 * COMP * PIECES],
        (
            whole_rows,
            local_rows,
            PADDED + 4,
            MEMBERS * COMP * PIECES,
            pltpu.SemaphoreType.DMA((len(given),)),
        ),
        "start",
        4,
        far=range(1, len(given) + 1),
    )
    x, donor, lower, upper, source, pivot, coupling, iblank = given
    fixed = (source, pivot, lower, upper, coupling, iblank)
    sent, scaled, starts = call(
        functools.partial(solve_kernel, count),
        (x, *near, *fixed, donated, maps, outer, share),
        (count * SLOT, state, 2 * COMP * PIECES),
        (state,),
        "solve",
        2,
    )
    shares = exchanged(sent, count)
    x, first, last = call(
        functools.partial(finish_kernel, count, SLOT),
        (shares, shares, members, lower, upper, maps, scaled, starts),
        (field, PIECES, PIECES),
        (state, entries),
        "finish",
        1,
    )

    near = both(x, x, "span") + both(last, first, "stream")
    (donated,) = call(donate_kernel, (x, donor), (state,), (), "donate", 2)
    sent, scaled, starts = call(
        functools.partial(solve_without, count),
        (x, *near, *fixed, donated, maps, outer),
        (count * VALUES, state, 2 * COMP * PIECES),
        (state,),
        "solve",
        2,
    )
    values = exchanged(sent, count)
    (x,) = call(
        functools.partial(finish_without, count, VALUES),
        (values, shares, members, lower, upper, maps, scaled, starts),
        (field,),
        (state, entries),
        "finish",
        1,
    )
    return x.reshape(iterate.shape)


def solution(mesh):
    placed = (
        P("normal", None, "span", "stream"),
        P("normal", None, "span", "stream"),
        P("normal", None, None, "span", "stream"),
        P("normal", None, None, "span", "stream"),
        P("normal", None, None, "span", "stream"),
        P(None, "normal", None, None, "span", "stream"),
        P("normal", "span", "stream"),
        P("normal", "span", "stream"),
    )
    return jax.shard_map(
        per_device,
        mesh=mesh,
        in_specs=placed,
        out_specs=P("normal", None, "span", "stream"),
        check_vma=False,
    )
```

```python
import functools

import jax
import jax.numpy as jnp
from jax import lax
from jax.experimental import pallas as pl
from jax.experimental.pallas import tpu as pltpu
from jax.sharding import PartitionSpec as P

COMP = 5
BLOCK = COMP * COMP
PIECES = 8
LANES = 128
STEPS = 6
POINTS = PIECES * STEPS
SIZES = range(COMP)
FWD0, FWD1, FWD2, BWD0, BWD1, BWD2, FOLD, HEAD, FROM_Y, FROM_X = range(10)
MAPS = 10
ROWS = 3 * BLOCK
VALUES = 2 * COMP
MEMBERS = 4
PADDED = 76
SHARE = PADDED // MEMBERS
SLOT = VALUES + SHARE
VMEM = pl.BlockSpec(memory_space=pltpu.VMEM)


def vector_at(ref, step):
    return [ref[pl.ds(step * COMP + c, PIECES, stride=STEPS * COMP), :] for c in SIZES]


def block_at(ref, step, base=0):
    start = base + step * BLOCK
    return [
        [ref[pl.ds(start + c * COMP + e, PIECES, stride=STEPS * BLOCK), :] for e in SIZES]
        for c in SIZES
    ]


def packed_at(ref, step):
    return [ref[pl.ds((step * COMP + c) * PIECES, PIECES), :] for c in SIZES]


def put_packed(ref, step, value):
    for c in SIZES:
        ref[pl.ds((step * COMP + c) * PIECES, PIECES), :] = value[c]


def map_at(ref, which):
    return [
        [ref[pl.ds(((which * COMP + c) * COMP + e) * PIECES, PIECES), :] for e in SIZES]
        for c in SIZES
    ]


def put_map(ref, which, value):
    for c in SIZES:
        for e in SIZES:
            ref[pl.ds(((which * COMP + c) * COMP + e) * PIECES, PIECES), :] = value[c][e]


def total(terms):
    while len(terms) > 1:
        terms = [sum(terms[k : k + 2][1:], terms[k]) for k in range(0, len(terms), 2)]
    return terms[0]


def times(block, vector):
    return [total([block[c][e] * vector[e] for e in SIZES]) for c in SIZES]


def product(left, right):
    return [
        [total([left[c][k] * right[k][e] for k in SIZES]) for e in SIZES] for c in SIZES
    ]


def each(function, *maps):
    return [[function(*(m[c][e] for m in maps)) for e in SIZES] for c in SIZES]


def add(left, right):
    return [a + b for a, b in zip(left, right)]


def less(left, right):
    return [a - b for a, b in zip(left, right)]


def moved(value, steps):
    return pltpu.roll(value, steps % PIECES, 0)


def donate(x_ref, donor_ref, donated_ref):
    lanes, rows = [], []
    for step in range(STEPS):
        place = donor_ref[pl.ds(step, PIECES, stride=STEPS), :]
        lanes.append(place & (LANES - 1))
        rows.append(place >> 7)

    zero = jnp.zeros((PIECES, LANES), jnp.float32)
    for step in range(STEPS):
        found = [zero] * COMP
        for row in range(POINTS):
            here = rows[step] == row
            for c in SIZES:
                line = jnp.broadcast_to(x_ref[pl.ds(row * COMP + c, 1), :], (PIECES, LANES))
                picked = jnp.take_along_axis(line, lanes[step], axis=1, mode="promise_in_bounds")
                found[c] = jnp.where(here, picked, found[c])
        put_packed(donated_ref, step, found)


def donate_kernel(x_ref, donor_ref, donated_ref):
    donate(x_ref, donor_ref, donated_ref)


def edges_of(ref):
    lane = lax.broadcasted_iota(jnp.int32, (PIECES, LANES), 1)
    first = last = jnp.zeros((PIECES, LANES), jnp.float32)
    for step in range(STEPS):
        for c, value in enumerate(vector_at(ref, step)):
            here = lane == step * COMP + c
            first = jnp.where(here, jnp.broadcast_to(value[:, :1], (PIECES, LANES)), first)
            last = jnp.where(here, jnp.broadcast_to(value[:, -1:], (PIECES, LANES)), last)
    return first, last


def summary_kernel(*refs):
    given, results, kept, (maps_ref, local_ref, moves) = refs[:3], refs[3:6], refs[6:12], refs[12:]
    coming = [pltpu.make_async_copy(a, b, moves.at[k]) for k, (a, b) in enumerate(zip(given, kept))]
    leaving = [
        pltpu.make_async_copy(a, b, moves.at[3 + k]) for k, (a, b) in enumerate(zip(kept[3:], results))
    ]
    x_ref, lower_ref, upper_ref, first_ref, last_ref, whole_ref = kept
    for copy in coming:
        copy.start()
    coming[0].wait()
    first_ref[...], last_ref[...] = edges_of(x_ref)
    for copy in leaving[:2]:
        copy.start()
    for copy in coming[1:]:
        copy.wait()
    make_maps(lower_ref, upper_ref, maps_ref, whole_ref, local_ref)
    leaving[2].start()
    for copy in leaving:
        copy.wait()


def start_kernel(*refs):
    members_ref, given, kept = refs[0], refs[1:9], refs[9:17]
    donated_ref, maps_ref, share_ref, outer_ref = refs[17:21]
    whole_ref, local_ref, group_ref, work_ref, arrived = refs[21:]
    copies = [
        pltpu.make_async_copy(a, b, arrived.at[k]) for k, (a, b) in enumerate(zip(given, kept))
    ]
    for copy in copies:
        copy.start()
    x_ref, donor_ref, lower_ref, upper_ref = kept[:4]
    group_maps(members_ref, share_ref, outer_ref, group_ref, work_ref)
    for copy in copies[:2]:
        copy.wait()
    donate(x_ref, donor_ref, donated_ref)
    for copy in copies[2:4]:
        copy.wait()
    make_maps(lower_ref, upper_ref, maps_ref, whole_ref, local_ref)
    for copy in copies[4:]:
        copy.wait()


def put_whole(ref, at, row):
    for member in range(MEMBERS):
        ref[pl.ds(member * PADDED + at, 1), :] = row


def make_maps(lower_ref, upper_ref, maps_ref, whole_ref, local_ref):
    piece = lax.broadcasted_iota(jnp.int32, (PIECES, LANES), 0)
    one = jnp.ones((PIECES, LANES), jnp.float32)
    zero = jnp.zeros((PIECES, LANES), jnp.float32)
    eye = [[one if c == e else zero for e in SIZES] for c in SIZES]

    def pack(value):
        return tuple(value[c][e] for c in SIZES for e in SIZES)

    def unpack(flat):
        return [list(flat[c * COMP : (c + 1) * COMP]) for c in SIZES]

    first = each(lambda a: -a, block_at(lower_ref, 0))
    put_map(local_ref, 0, first)

    def forward(step, state):
        block = block_at(lower_ref, step)
        state = each(lambda a: -a, product(block, unpack(state)))
        put_map(local_ref, step, state)
        return pack(state)

    ahead = unpack(lax.fori_loop(1, STEPS, forward, pack(first), unroll=True))

    def backward(count, carry):
        behind, fold = unpack(carry[:BLOCK]), unpack(carry[BLOCK:])
        step = STEPS - 1 - count
        block = block_at(upper_ref, step)
        behind = each(lambda a: -a, product(block, behind))
        fold = each(lambda a, b: a - b, map_at(local_ref, step), product(block, fold))
        return pack(behind) + pack(fold)

    last = block_at(upper_ref, STEPS - 1)
    start = pack(each(lambda a: -a, last)) + pack(map_at(local_ref, STEPS - 1))
    carry = lax.fori_loop(1, STEPS, backward, start, unroll=True)
    behind, fold = unpack(carry[:BLOCK]), unpack(carry[BLOCK:])
    put_map(maps_ref, FOLD, fold)

    window = ahead
    for level, shift in enumerate((1, 2, 4)):
        inside = piece >= shift
        put_map(maps_ref, FWD0 + level, each(lambda a: jnp.where(inside, a, 0.0), window))
        longer = product(window, each(lambda a: moved(a, shift), window))
        window = each(lambda a, b: jnp.where(inside, a, b), longer, window)
    head = each(lambda a, b: jnp.where(piece == 0, b, moved(a, 1)), window, eye)
    put_map(maps_ref, HEAD, head)
    for c in SIZES:
        for e in SIZES:
            put_whole(whole_ref, c * COMP + e, window[c][e][PIECES - 1 :, :])

    window = behind
    response = product(fold, head)
    for level, shift in enumerate((1, 2, 4)):
        inside = piece < PIECES - shift
        masked = each(lambda a: jnp.where(inside, a, 0.0), window)
        put_map(maps_ref, BWD0 + level, masked)
        response = each(
            lambda a, b: a + b,
            response,
            product(masked, each(lambda a: moved(a, -shift), response)),
        )
        longer = product(window, each(lambda a: moved(a, -shift), window))
        window = each(lambda a, b: jnp.where(inside, a, b), longer, window)
    final = piece == PIECES - 1
    put_map(maps_ref, FROM_Y, each(lambda a: jnp.where(final, 0.0, moved(a, -1)), response))
    put_map(maps_ref, FROM_X, each(lambda a, b: jnp.where(final, b, moved(a, -1)), window, eye))
    for c in SIZES:
        for e in SIZES:
            at = c * COMP + e
            put_whole(whole_ref, BLOCK + at, response[c][e][:1, :])
            put_whole(whole_ref, 2 * BLOCK + at, window[c][e][:1, :])
    put_whole(whole_ref, ROWS, jnp.zeros((1, LANES), jnp.float32))


def solve_kernel(
    count,
    x_ref,
    below_ref,
    above_ref,
    left_ref,
    right_ref,
    source_ref,
    pivot_ref,
    lower_ref,
    upper_ref,
    coupling_ref,
    iblank_ref,
    donated_ref,
    maps_ref,
    outer_ref,
    share_ref,
    sent_ref,
    scaled_ref,
    starts_ref,
    states_ref,
):
    lane = lax.broadcasted_iota(jnp.int32, (PIECES, LANES), 1)
    piece = lax.broadcasted_iota(jnp.int32, (PIECES, LANES), 0)
    zero = jnp.zeros((PIECES, LANES), jnp.float32)

    def forward(step, state):
        x = vector_at(x_ref, step)
        before, after = [], []
        for c in SIZES:
            place = jnp.full((PIECES, LANES), step * COMP + c, jnp.int32)
            for out, edges_ref, turn, at in (
                (before, left_ref, 1, 0),
                (after, right_ref, LANES - 1, LANES - 1),
            ):
                edge = jnp.take_along_axis(edges_ref[...], place, axis=1, mode="promise_in_bounds")
                out.append(jnp.where(lane == at, edge, pltpu.roll(x[c], turn, 1)))
        near = [vector_at(below_ref, step), vector_at(above_ref, step), before, after]
        rhs = vector_at(source_ref, step)
        for direc in range(4):
            block = block_at(coupling_ref, step, direc * POINTS * BLOCK)
            for c in SIZES:
                rhs[c] = rhs[c] - total([block[e][c] * near[direc][e] for e in SIZES])
        flag = iblank_ref[pl.ds(step, PIECES, stride=STEPS), :]
        donated = packed_at(donated_ref, step)
        rhs = [
            jnp.where(flag == 0, 0.0, a + jnp.where(flag == 2, b, 0.0))
            for a, b in zip(rhs, donated)
        ]
        scaled = times(block_at(pivot_ref, step), rhs)
        put_packed(scaled_ref, step, scaled)
        state = less(scaled, times(block_at(lower_ref, step), state))
        put_packed(states_ref, step, state)
        return tuple(state)

    ahead = list(lax.fori_loop(0, STEPS, forward, (zero,) * COMP, unroll=True))

    def backward(count, state):
        step = STEPS - 1 - count
        y = packed_at(states_ref, step)
        return tuple(less(y, times(block_at(upper_ref, step), state)))

    behind = list(lax.fori_loop(0, STEPS, backward, (zero,) * COMP, unroll=True))

    for level, shift in enumerate((1, 2, 4)):
        ahead = add(ahead, times(map_at(maps_ref, FWD0 + level), [moved(a, shift) for a in ahead]))
    entry = [jnp.where(piece == 0, 0.0, moved(a, 1)) for a in ahead]
    behind = add(behind, times(map_at(maps_ref, FOLD), entry))
    for level, shift in enumerate((1, 2, 4)):
        behind = add(
            behind, times(map_at(maps_ref, BWD0 + level), [moved(a, -shift) for a in behind])
        )
    put_packed(starts_ref, 0, entry)
    put_packed(
        starts_ref, 1, [jnp.where(piece == PIECES - 1, 0.0, moved(a, -1)) for a in behind]
    )
    y_out = [jnp.broadcast_to(a[PIECES - 1 :, :], (COMP, LANES)) for a in ahead]
    x_out = [jnp.broadcast_to(a[:1, :], (COMP, LANES)) for a in behind]
    row = lax.broadcasted_iota(jnp.int32, (COMP, LANES), 0)

    def stacked(rows):
        out = rows[0]
        for c in SIZES[1:]:
            out = jnp.where(row == c, rows[c], out)
        return out

    def outer(which, rows):
        return total([outer_ref[pl.ds((which * COMP + e) * PIECES, COMP), :] * rows[e] for e in SIZES])

    inside = stacked(y_out), stacked(x_out)
    outside = outer(0, y_out), outer(1, y_out) + outer(2, x_out)
    mine = lax.axis_index("normal") // MEMBERS
    slot = VALUES if share_ref is None else SLOT
    for device in range(count):
        same = mine == device // MEMBERS
        for k in range(2):
            at = device * slot + k * COMP
            sent_ref[pl.ds(at, COMP), :] = jnp.where(same, inside[k], outside[k])
        if share_ref is not None:
            sent_ref[pl.ds(device * slot + VALUES, SHARE), :] = share_ref[pl.ds(0, SHARE), :]


def solve_without(count, *refs):
    solve_kernel(count, *refs[:14], None, *refs[14:])


def group_maps(members_ref, share_ref, outer_ref, whole_ref, work_ref):
    own = lax.rem(lax.axis_index("normal"), MEMBERS)
    row = lax.broadcasted_iota(jnp.int32, (COMP, LANES), 0)
    eye = [jnp.where(row == e, 1.0, 0.0) for e in SIZES]
    none = [jnp.zeros((COMP, LANES), jnp.float32)] * COMP

    def given(member, which):
        base = member * PADDED + which * BLOCK
        columns = [members_ref[pl.ds(base + e, COMP, stride=COMP), :] for e in SIZES]
        return columns, lambda k, e: members_ref[pl.ds(base + k * COMP + e, 1), :]

    def kept(columns, place):
        for e in SIZES:
            work_ref[pl.ds((place * COMP + e) * PIECES, COMP), :] = columns[e]
        return lambda k, e: work_ref[pl.ds((place * COMP + e) * PIECES + k, 1), :]

    def multiply(columns, element):
        return [total([columns[k] * element(k, e) for k in SIZES]) for e in SIZES]

    def chosen(options):
        out = options[-1]
        for member in range(MEMBERS - 1):
            out = [jnp.where(own == member, a, b) for a, b in zip(options[member], out)]
        return out

    onward, across = [given(MEMBERS - 1, 0)[0]], [given(MEMBERS - 1, 1)[0]]
    for member in range(MEMBERS - 2, -1, -1):
        forward = given(member, 0)[1]
        onward.insert(0, multiply(onward[0], forward))
        inner = kept(multiply(across[0], forward), member)
        across.insert(0, add(given(member, 1)[0], multiply(given(member, 2)[0], inner)))
    back = [eye, given(0, 2)[0]]
    for member in range(1, MEMBERS):
        back.append(multiply(back[-1], given(member, 2)[1]))
    mixed = multiply(
        chosen(back[1:MEMBERS] + [none]), kept(chosen(across[1:] + [none]), MEMBERS - 1)
    )
    for k, columns in enumerate((chosen(onward[1:] + [eye]), mixed, chosen(back[:MEMBERS]))):
        for e in SIZES:
            outer_ref[pl.ds((k * COMP + e) * PIECES, COMP), :] = columns[e]
    for k, columns in enumerate((onward[0], across[0], back[MEMBERS])):
        for e in SIZES:
            whole_ref[pl.ds(k * BLOCK + e, COMP, stride=COMP), :] = columns[e]
    whole_ref[pl.ds(ROWS, 1), :] = jnp.zeros((1, LANES), jnp.float32)
    share_ref[pl.ds(0, SHARE), :] = whole_ref[pl.ds(own * SHARE, SHARE), :]


def finish_kernel(
    count,
    slot,
    values_ref,
    shares_ref,
    members_ref,
    lower_ref,
    upper_ref,
    maps_ref,
    scaled_ref,
    starts_ref,
    out_ref,
    first_ref,
    last_ref,
    states_ref,
    entry_ref,
):
    me = lax.axis_index("normal")
    mine, own = me // MEMBERS, lax.rem(me, MEMBERS)
    groups = count // MEMBERS

    def group_map(group, which):
        def row(at):
            place = (group * MEMBERS + at // SHARE) * SLOT + VALUES + at % SHARE
            return shares_ref[pl.ds(place, 1), :]

        return [[row((which * COMP + c) * COMP + e) for e in SIZES] for c in SIZES]

    def member_map(member, which):
        base = member * PADDED + which * BLOCK
        return [[members_ref[pl.ds(base + c * COMP + e, 1), :] for e in SIZES] for c in SIZES]

    def value(device, which):
        return [values_ref[pl.ds(device * slot + which * COMP + c, 1), :] for c in SIZES]

    def group_value(group, which):
        parts = [value(group * MEMBERS + member, which) for member in range(MEMBERS)]
        return [total([part[c] for part in parts]) for c in SIZES]

    def put_entry(at, state):
        for c in SIZES:
            entry_ref[pl.ds(at * PIECES + c, 1), :] = state[c]

    def entry(at):
        return [entry_ref[pl.ds(at * PIECES + c, 1), :] for c in SIZES]

    none = (jnp.zeros((1, LANES), jnp.float32),) * COMP

    def over_group(group, state):
        put_entry(group, state)
        return tuple(add(group_value(group, 0), times(group_map(group, 0), list(state))))

    state = lax.fori_loop(0, mine, over_group, none)
    for member in range(MEMBERS):
        put_entry(groups + member, state)
        state = add(value(mine * MEMBERS + member, 0), times(member_map(member, 0), list(state)))
    lax.fori_loop(mine + 1, groups, over_group, tuple(state))

    def back_over_group(step, state):
        group = groups - 1 - step
        inner = add(group_value(group, 1), times(group_map(group, 1), entry(group)))
        return tuple(add(inner, times(group_map(group, 2), list(state))))

    state = lax.fori_loop(0, groups - 1 - mine, back_over_group, none)

    def back_over_member(step, state):
        member = MEMBERS - 1 - step
        inner = add(
            value(mine * MEMBERS + member, 1), times(member_map(member, 1), entry(groups + member))
        )
        return tuple(add(inner, times(member_map(member, 2), list(state))))

    x_in = lax.fori_loop(0, MEMBERS - 1 - own, back_over_member, state)

    y_in = [jnp.broadcast_to(a, (PIECES, LANES)) for a in entry(groups + own)]
    x_in = [jnp.broadcast_to(a, (PIECES, LANES)) for a in x_in]

    y_start = add(packed_at(starts_ref, 0), times(map_at(maps_ref, HEAD), y_in))
    x_start = add(packed_at(starts_ref, 1), times(map_at(maps_ref, FROM_Y), y_in))
    x_start = add(x_start, times(map_at(maps_ref, FROM_X), x_in))

    def ahead(step, state):
        state = less(packed_at(scaled_ref, step), times(block_at(lower_ref, step), list(state)))
        put_packed(states_ref, step, state)
        return tuple(state)

    lax.fori_loop(0, STEPS, ahead, tuple(y_start), unroll=True)

    def behind(turn, state):
        step = STEPS - 1 - turn
        state = less(packed_at(states_ref, step), times(block_at(upper_ref, step), list(state)))
        for c in SIZES:
            out_ref[pl.ds(step * COMP + c, PIECES, stride=STEPS * COMP), :] = state[c]
        return tuple(state)

    lax.fori_loop(0, STEPS, behind, tuple(x_start), unroll=True)
    if first_ref is not None:
        first_ref[...], last_ref[...] = edges_of(out_ref)


def finish_without(count, slot, *refs):
    finish_kernel(count, slot, *refs[:9], None, None, *refs[9:])


def floats(rows):
    return jax.ShapeDtypeStruct((rows, LANES), jnp.float32)


def scratch(rows):
    return pltpu.VMEM((rows, LANES), jnp.float32)


def call(kernel, inputs, outputs, scratches, name, micros, far=()):
    hbm = pl.BlockSpec(memory_space=pltpu.HBM)
    places = range(len(inputs) + len(outputs))
    specs = [hbm if k in far else VMEM for k in places]
    inputs = [
        pltpu.with_memory_space_constraint(a, pltpu.HBM) if k in far else a
        for k, a in enumerate(inputs)
    ]
    return pl.pallas_call(
        kernel,
        out_shape=[floats(a) if isinstance(a, int) else a for a in outputs],
        in_specs=specs[: len(inputs)],
        out_specs=specs[len(inputs) :],
        scratch_shapes=[scratch(a) if isinstance(a, int) else a for a in scratches],
        compiler_params=pltpu.CompilerParams(vmem_limit_bytes=16 << 20),
        cost_estimate=pl.CostEstimate(
            flops=0, bytes_accessed=int(micros * 3.0e6), transcendentals=0
        ),
        name=name,
    )(*inputs)


def ring(count, step):
    return [(i, (i + step) % count) for i in range(count)]


def per_device(iterate, source, pivot, lower, upper, coupling, iblank, donor):
    count = lax.axis_size("normal")
    x = iterate.reshape(-1, LANES)
    source, pivot, lower, upper, coupling, iblank, donor = (
        a.reshape(-1, LANES) for a in (source, pivot, lower, upper, coupling, iblank, donor)
    )
    field = POINTS * COMP
    state = STEPS * COMP * PIECES

    def both(up, down, axis):
        size = lax.axis_size(axis)
        return [lax.ppermute(up, axis, ring(size, 1)), lax.ppermute(down, axis, ring(size, -1))]

    def exchanged(rows, parts, groups=None):
        rows = rows.reshape(parts, -1, 1, LANES)
        return lax.all_to_all(rows, "normal", 0, 0, axis_index_groups=groups).reshape(-1, LANES)

    maps_rows = MAPS * BLOCK * PIECES
    local_rows = STEPS * BLOCK * PIECES
    whole_rows = MEMBERS * PADDED
    entries = (count // MEMBERS + MEMBERS) * PIECES

    first, last, whole = call(
        summary_kernel,
        (x, lower, upper),
        (PIECES, PIECES, whole_rows),
        (
            x.shape[0],
            lower.shape[0],
            upper.shape[0],
            PIECES,
            PIECES,
            whole_rows,
            maps_rows,
            local_rows,
            pltpu.SemaphoreType.DMA((6,)),
        ),
        "summary",
        2,
        far=range(6),
    )
    groups = [list(range(k, k + MEMBERS)) for k in range(0, count, MEMBERS)]
    members = exchanged(whole, MEMBERS, groups)
    near = both(x, x, "span") + both(last, first, "stream")
    given = (x, donor, lower, upper, source, pivot, coupling, iblank)
    *given, donated, maps, share, outer = call(
        start_kernel,
        (members, *given),
        [jax.ShapeDtypeStruct(a.shape, a.dtype) for a in given]
        + [state, maps_rows, 24, 3 * COMP * PIECES],
        (
            whole_rows,
            local_rows,
            PADDED + 4,
            MEMBERS * COMP * PIECES,
            pltpu.SemaphoreType.DMA((len(given),)),
        ),
        "start",
        4,
        far=range(1, len(given) + 1),
    )
    x, donor, lower, upper, source, pivot, coupling, iblank = given
    fixed = (source, pivot, lower, upper, coupling, iblank)
    sent, scaled, starts = call(
        functools.partial(solve_kernel, count),
        (x, *near, *fixed, donated, maps, outer, share),
        (count * SLOT, state, 2 * COMP * PIECES),
        (state,),
        "solve",
        2,
    )
    shares = exchanged(sent, count)
    x, first, last = call(
        functools.partial(finish_kernel, count, SLOT),
        (shares, shares, members, lower, upper, maps, scaled, starts),
        (field, PIECES, PIECES),
        (state, entries),
        "finish",
        1,
    )

    near = both(x, x, "span") + both(last, first, "stream")
    (donated,) = call(donate_kernel, (x, donor), (state,), (), "donate", 2)
    sent, scaled, starts = call(
        functools.partial(solve_without, count),
        (x, *near, *fixed, donated, maps, outer),
        (count * VALUES, state, 2 * COMP * PIECES),
        (state,),
        "solve",
        2,
    )
    values = exchanged(sent, count)
    (x,) = call(
        functools.partial(finish_without, count, VALUES),
        (values, shares, members, lower, upper, maps, scaled, starts),
        (field,),
        (state, entries),
        "finish",
        1,
    )
    return x.reshape(iterate.shape)


def solution(mesh):
    placed = (
        P("normal", None, "span", "stream"),
        P("normal", None, "span", "stream"),
        P("normal", None, None, "span", "stream"),
        P("normal", None, None, "span", "stream"),
        P("normal", None, None, "span", "stream"),
        P(None, "normal", None, None, "span", "stream"),
        P("normal", "span", "stream"),
        P("normal", "span", "stream"),
    )
    return jax.shard_map(
        per_device,
        mesh=mesh,
        in_specs=placed,
        out_specs=P("normal", None, "span", "stream"),
        check_vma=False,
    )
```
